512 devices in a mesh: seq: 64 (over z, x), kv: 8 (over y, core).
Axes of the slice: x: 4, y: 4, z: 16, core: 2. Of those that a mesh axis runs over, the one named last changes fastest.
Arguments:
- queries: bfloat16 [16384, 8192], P(('seq', 'kv')), may hold values from -5 to 5
- keys: bfloat16 [16384, 1024], P(('seq', 'kv')), may hold values from -5 to 5
- values: bfloat16 [16384, 1024], P(('seq', 'kv')), may hold values from -6 to 6
- grad_out: bfloat16 [16384, 8192], P(('seq', 'kv')), may hold values from -6 to 6
- lengths: int32 [32], replicated, may hold values from 1 to 1536, 16384 in all
Outputs:
- attended: bfloat16 [16384, 8192], P(('seq', 'kv'))
- grad_queries: bfloat16 [16384, 8192], P(('seq', 'kv'))
- grad_keys: bfloat16 [16384, 1024], P(('seq', 'kv'))
- grad_values: bfloat16 [16384, 1024], P(('seq', 'kv'))
The draws below stay inside these ranges and needn't reach their ends.
Inputs may be any that keep to these rules, and one draw needn't show every extreme that they name: lengths sum to 16384; the longest is exactly 1536.
All inputs are finite; a program needn't handle non-finite values.
Results may differ from the reference program's by a relative error of at most 0.025.
Values may be sent and summed in bfloat16 or wider, within the bound.
A program may use at most 64 MiB of HBM per device.

```python
import math
import jax
import jax.numpy as jnp
import numpy as np
from jax import lax

HD = 128
GROUP = 8
TOK_DEV = 256
WIN = 6
DOCS = 32
KVH = 8
QH = 64
TOKENS = 16384
DOC_MOST = 1536
N_SEQ = 64


def draw_queries(key, part):
    key = jax.random.fold_in(key, 1)
    return jnp.clip(jax.random.normal(key, (TOKENS, QH * HD)), -5.0, 5.0).astype(jnp.bfloat16)


def draw_keys(key, part):
    key = jax.random.fold_in(key, 2)
    return jnp.clip(jax.random.normal(key, (TOKENS, KVH * HD)), -5.0, 5.0).astype(jnp.bfloat16)


def block_levels(key, shape, split, low, largest):
    def one(dim, shards_of):
        draws = jax.random.uniform(jax.random.fold_in(jax.random.fold_in(key, 6), dim), (shards_of,), jnp.float32, low / len(split), largest / len(split))
        return jnp.repeat(jnp.exp(draws), shape[dim] // shards_of).reshape((-1,) + (1,) * (len(shape) - dim - 1))

    factor_of = one(*split[0])
    for cut in split[1:]:
        factor_of = factor_of * one(*cut)
    return factor_of


def split_up(amount, total, most, lean):
    portions = [(1 << 20) // math.isqrt(rank ** lean) + 1 for rank in range(2, amount + 1)]
    spare, given = total - most - (amount - 1), [1] * (amount - 1)
    while spare > 0:
        candidates = [i for i in range(amount - 1) if given[i] < most]
        pool, budget = sum([portions[i] for i in candidates]), spare
        for i in candidates:
            addition = min(most - given[i], max(1, budget * portions[i] // pool), spare)
            given[i] = given[i] + addition
            spare = spare - addition
    return np.array([most] + given)


def ragged_sizes(own_key, count, total, reach, lean):
    if count == 2:
        one = jax.random.randint(own_key, (), max(1, total - reach), min(reach, total - 1) + 1)
        return jnp.stack([one, total - one])
    sizes = jnp.asarray(split_up(count, total, reach, lean), jnp.int32)
    twos = (count - 1) // 2
    donor, taker = sizes[1:1 + 2 * twos:2], sizes[2:2 + 2 * twos:2]
    slack = jnp.minimum(donor - 1, reach - taker)
    moved = jax.random.randint(jax.random.fold_in(own_key, 1), (twos,), 0, 1 << 20) % (slack + 1)
    sizes = sizes.at[1:1 + 2 * twos:2].set(donor - moved).at[2:2 + 2 * twos:2].set(taker + moved)
    return sizes[jax.random.permutation(jax.random.fold_in(own_key, 2), count)]


def centred(stream_key, shape, width, reach, cuts=(), held_as=jnp.bfloat16):
    drawn = jax.random.normal(stream_key, shape, jnp.float32) * width
    if len(cuts) > 0:
        drawn = block_levels(stream_key, shape, cuts, -0.22, 0.18) * drawn
    return jnp.clip(drawn, min=-reach, max=reach).astype(held_as)


def setup_inputs(seed: int = 0) -> dict:
    arg_keys = jax.random.split(jax.random.key(seed), 6)
    return {
        "queries": draw_queries(jax.random.fold_in(arg_keys[5], 71), 0),
        "keys": draw_keys(jax.random.fold_in(arg_keys[5], 71), 0),
        "values": centred(arg_keys[2], (TOKENS, KVH * HD), 1.0, 6.0, ((0, 512),)),
        "grad_out": centred(arg_keys[3], (TOKENS, QH * HD), 1.0, 6.0, ((0, 512),)),
        "lengths": ragged_sizes(arg_keys[4], DOCS, TOKENS, DOC_MOST, 2).astype(jnp.int32),
    }


def segment_of(positions, ends):
    counted = jnp.sum((positions[:, None] >= ends[None, :]).astype(jnp.int32), axis=1)
    return jnp.where(positions >= 0, counted, -1)


def reference(queries, keys, values, grad_out, lengths):
    softmax_scale = HD ** -0.5
    window = (WIN + 1) * TOK_DEV
    reach_back = WIN * TOK_DEV
    ends = jnp.cumsum(lengths).astype(jnp.int32)
    query_grid = queries.reshape(TOKENS, KVH, GROUP, HD)
    grad_grid = grad_out.reshape(TOKENS, KVH, GROUP, HD)
    padding = jnp.zeros((reach_back, KVH * HD), jnp.bfloat16)
    key_padded = jnp.concatenate([padding, keys], axis=0).reshape(TOKENS + reach_back, KVH, HD)
    val_padded = jnp.concatenate([padding, values], axis=0).reshape(TOKENS + reach_back, KVH, HD)

    def block_step(carry, block_index):
        key_grad, val_grad = carry
        start = (block_index * TOK_DEV).astype(jnp.int32)
        query_block = lax.dynamic_slice_in_dim(query_grid, start, TOK_DEV, 0).astype(jnp.float32)
        grad_block = lax.dynamic_slice_in_dim(grad_grid, start, TOK_DEV, 0).astype(jnp.float32)
        key_block = lax.dynamic_slice_in_dim(key_padded, start, window, 0).astype(jnp.float32)
        val_block = lax.dynamic_slice_in_dim(val_padded, start, window, 0).astype(jnp.float32)
        query_pos = start + jnp.arange(TOK_DEV, dtype=jnp.int32)
        key_pos = start - reach_back + jnp.arange(window, dtype=jnp.int32)
        allowed = (segment_of(key_pos, ends)[None, :] == segment_of(query_pos, ends)[:, None]) & (key_pos[None, :] <= query_pos[:, None]) & (key_pos[None, :] >= 0)
        scores = jnp.einsum("qhgd,khd->hgqk", query_block, key_block) * softmax_scale
        scores = jnp.where(allowed, scores, -jnp.inf)
        row_max = jnp.max(scores, axis=-1, keepdims=True)
        log_total = row_max + jnp.log(jnp.sum(jnp.exp(scores - row_max), axis=-1, keepdims=True))
        weights = jnp.where(allowed, jnp.exp(scores - log_total), 0.0)
        weights_low = lax.optimization_barrier(weights.astype(jnp.bfloat16)).astype(jnp.float32)
        attended = jnp.einsum("hgqk,khd->qhgd", weights_low, val_block).astype(jnp.bfloat16)
        delta = jnp.sum(grad_block * attended.astype(jnp.float32), axis=-1)
        grad_weights = jnp.einsum("qhgd,khd->hgqk", grad_block, val_block)
        grad_scores = weights * (grad_weights - jnp.transpose(delta, (1, 2, 0))[..., None])
        grad_low = lax.optimization_barrier(grad_scores.astype(jnp.bfloat16)).astype(jnp.float32)
        grad_query = (softmax_scale * jnp.einsum("hgqk,khd->qhgd", grad_low, key_block)).astype(jnp.bfloat16)
        key_part = jnp.einsum("hgqk,qhgd->khd", grad_low, query_block)
        val_part = jnp.einsum("hgqk,qhgd->khd", weights_low, grad_block)
        key_grad = lax.dynamic_update_slice_in_dim(key_grad, lax.dynamic_slice_in_dim(key_grad, start, window, 0) + key_part, start, 0)
        val_grad = lax.dynamic_update_slice_in_dim(val_grad, lax.dynamic_slice_in_dim(val_grad, start, window, 0) + val_part, start, 0)
        return (key_grad, val_grad), (attended, grad_query)

    zeros_init = jnp.zeros((TOKENS + reach_back, KVH, HD), jnp.float32)
    (key_grad, val_grad), (attended, grad_query) = lax.scan(block_step, (zeros_init, zeros_init), jnp.arange(N_SEQ, dtype=jnp.int32))
    attended = attended.reshape(TOKENS, QH * HD)
    grad_query = grad_query.reshape(TOKENS, QH * HD)
    grad_keys = (softmax_scale * key_grad[reach_back:]).astype(jnp.bfloat16).reshape(TOKENS, KVH * HD)
    grad_values = val_grad[reach_back:].astype(jnp.bfloat16).reshape(TOKENS, KVH * HD)
    return attended, grad_query, grad_keys, grad_values
```

```python
import functools

import jax
import jax.numpy as jnp
from jax import lax
from jax.experimental import pallas as pl
from jax.experimental.pallas import tpu as pltpu
from jax.sharding import PartitionSpec as P

HD = 128
GROUP = 8
WIN = 6
MESH = pl.DeviceIdType.MESH
SCALE = HD ** (-0.5)
SCALE2 = SCALE * 1.4426950408889634
MASKED = -1e30
F32 = jnp.float32
BF16 = jnp.bfloat16


def any_spec():
    return pl.BlockSpec(memory_space=pl.ANY)


def vmem_spec():
    return pl.BlockSpec(memory_space=pltpu.VMEM)


def remote(src, dst, send, recv, peer):
    return pltpu.make_async_remote_copy(
        src_ref=src, dst_ref=dst, send_sem=send, recv_sem=recv, device_id=peer, device_id_type=MESH
    )


def gather_kernel(nk, ns, q_ref, k_ref, v_ref, g_ref, q_out, g_out, kw, vw, own_sem, send_kv, recv_kv, send_win, recv_win):
    me = lax.axis_index("kv")
    spot = lax.axis_index("seq")
    tok = q_ref.shape[0]
    rows = tok * nk
    width = q_ref.shape[1] // nk
    peers = [lax.rem(me + o, nk) for o in range(1, nk)]
    ahead = [lax.rem(spot + d, ns) for d in range(1, WIN + 1)]
    behind = [lax.rem(spot + ns - d, ns) for d in range(1, WIN + 1)]

    barrier = pltpu.get_barrier_semaphore()
    for peer in peers:
        pl.semaphore_signal(barrier, inc=1, device_id={"kv": peer}, device_id_type=MESH)
    for peer in behind:
        pl.semaphore_signal(barrier, inc=1, device_id={"seq": peer}, device_id_type=MESH)
    pl.semaphore_wait(barrier, nk - 1 + WIN)

    mine = pl.ds(pl.multiple_of(me * tok, tok), tok)
    arrays = (
        (k_ref, kw.at[WIN], HD),
        (v_ref, vw.at[WIN], HD),
        (q_ref, q_out, width),
        (g_ref, g_out, width),
    )

    def piece(src, size, to):
        return src.at[:, pl.ds(pl.multiple_of(to * size, size), size)]

    copies = []
    locals_ = []
    for a, (src, dst, size) in enumerate(arrays):
        local = pltpu.make_async_copy(piece(src, size, me), dst.at[mine, :], own_sem.at[a])
        local.start()
        locals_.append(local)
        sent = []
        for o, peer in enumerate(peers):
            copy = remote(
                piece(src, size, peer), dst.at[mine, :], send_kv.at[a, o], recv_kv.at[a, o], {"kv": peer}
            )
            copy.start()
            sent.append(copy)
        copies.append(sent)
    far = []
    for a, win in enumerate((kw, vw)):
        locals_[a].wait()
        for copy in copies[a]:
            copy.wait_recv()
        for d in range(1, WIN + 1):
            copy = remote(
                win.at[WIN], win.at[WIN - d], send_win.at[a, d - 1], recv_win.at[a, d - 1], {"seq": ahead[d - 1]}
            )
            copy.start()
            far.append(copy)
    for a in (2, 3):
        locals_[a].wait()
        for copy in copies[a]:
            copy.wait_recv()
    for copy in far:
        copy.wait()
    for sent in copies:
        for copy in sent:
            copy.wait_send()


def gather(queries, keys, values, grad_out):
    nk, ns = lax.axis_size("kv"), lax.axis_size("seq")
    tok = queries.shape[0]
    rows = tok * nk
    width = queries.shape[1] // nk
    return pl.pallas_call(
        functools.partial(gather_kernel, nk, ns),
        out_shape=(
            jax.ShapeDtypeStruct((rows, width), BF16),
            jax.ShapeDtypeStruct((rows, width), BF16),
            jax.ShapeDtypeStruct((WIN + 1, rows, HD), BF16),
            jax.ShapeDtypeStruct((WIN + 1, rows, HD), BF16),
        ),
        in_specs=[any_spec()] * 4,
        out_specs=(vmem_spec(), vmem_spec(), vmem_spec(), vmem_spec()),
        scratch_shapes=[
            pltpu.SemaphoreType.DMA((4,)),
            pltpu.SemaphoreType.DMA((4, nk - 1)),
            pltpu.SemaphoreType.DMA((4, nk - 1)),
            pltpu.SemaphoreType.DMA((2, WIN)),
            pltpu.SemaphoreType.DMA((2, WIN)),
        ],
        compiler_params=pltpu.CompilerParams(
            collective_id=0, has_side_effects=True, vmem_limit_bytes=48 << 20
        ),
        name="gather",
    )(queries, keys, values, grad_out)


def dot(a, b):
    return jnp.dot(a, b, preferred_element_type=F32)


def dot_nt(a, b):
    return lax.dot_general(a, b, (((1,), (1,)), ((), ())), preferred_element_type=F32)


def fold(x, op):
    rows, cols = x.shape
    return op(x.reshape(rows // 8, 8, cols), axis=0)


def attend_kernel(
    first_ref, ends_ref, q_ref, g_ref, kw, vw, o_ref, dq_ref, dk_ref, dv_ref,
    bias, scores, probs, key_t, val_t, dk_acc, dv_acc,
):
    blocks, rows, _ = kw.shape
    first = first_ref[0]
    query_pos = first + lax.broadcasted_iota(jnp.int32, (1, rows), 1)
    start = jnp.zeros((1, rows), jnp.int32)
    for d in range(ends_ref.shape[0]):
        end = ends_ref[d]
        start = jnp.where(query_pos >= end, jnp.maximum(start, end), start)
    for b in range(blocks):
        key_pos = first + (b - WIN) * rows + lax.broadcasted_iota(jnp.int32, (rows, rows), 0)
        allowed = (key_pos >= start) & (key_pos <= query_pos)
        bias[b] = jnp.where(allowed, 0.0, MASKED)
        key_t[b] = kw[b].T
        val_t[b] = vw[b].T
        dk_acc[b] = jnp.zeros((rows, HD), F32)
        dv_acc[b] = jnp.zeros((rows, HD), F32)

    def step(h, carry):
        cols = pl.ds(pl.multiple_of(h * HD, HD), HD)
        qh = q_ref[:, cols]
        gh = g_ref[:, cols]
        top = jnp.full((8, rows), MASKED, F32)
        for b in range(blocks):
            s = dot_nt(kw[b], qh) + bias[b]
            scores[b] = s
            top = jnp.maximum(top, fold(s, jnp.max))
        top = jnp.max(top, axis=0, keepdims=True) * SCALE2
        total = jnp.zeros((8, rows), F32)
        out_t = jnp.zeros((HD, rows), F32)
        for b in range(blocks):
            p = jnp.exp2(scores[b] * SCALE2 - top)
            total = total + fold(p, jnp.sum)
            low = p.astype(BF16)
            probs[b] = low
            out_t = out_t + dot(val_t[b], low)
        over = 1.0 / jnp.sum(total, axis=0, keepdims=True)
        out_low = (out_t * over).T.astype(BF16)
        o_ref[:, cols] = out_low
        delta = jnp.sum((gh.astype(F32) * out_low.astype(F32)).T, axis=0, keepdims=True)
        over_col = jnp.broadcast_to(over, (HD, rows)).T
        qs = (qh.astype(F32) * over_col).astype(BF16)
        gs = (gh.astype(F32) * over_col).astype(BF16)
        dq_t = jnp.zeros((HD, rows), F32)
        for b in range(blocks):
            low = probs[b]
            ds = (low.astype(F32) * (dot_nt(vw[b], gh) - delta)).astype(BF16)
            dk_acc[b] += dot(ds, qs)
            dv_acc[b] += dot(low, gs)
            dq_t = dq_t + dot(key_t[b], ds)
        dq_ref[:, cols] = (dq_t * (over * SCALE)).T.astype(BF16)
        return carry

    lax.fori_loop(0, GROUP, step, 0)
    dk_ref[...] = dk_acc[...].astype(dk_ref.dtype)
    dv_ref[...] = dv_acc[...].astype(dv_ref.dtype)


def attend(q_loc, g_loc, kw, vw, first, ends):
    blocks, rows, _ = kw.shape
    smem = pl.BlockSpec(memory_space=pltpu.SMEM)
    return pl.pallas_call(
        attend_kernel,
        out_shape=(
            jax.ShapeDtypeStruct(q_loc.shape, BF16),
            jax.ShapeDtypeStruct(q_loc.shape, BF16),
            jax.ShapeDtypeStruct(kw.shape, BF16),
            jax.ShapeDtypeStruct(kw.shape, BF16),
        ),
        in_specs=[smem, smem] + [vmem_spec()] * 4,
        out_specs=(vmem_spec(),) * 4,
        scratch_shapes=[
            pltpu.VMEM((blocks, rows, rows), F32),
            pltpu.VMEM((blocks, rows, rows), F32),
            pltpu.VMEM((blocks, rows, rows), BF16),
            pltpu.VMEM((blocks, HD, rows), BF16),
            pltpu.VMEM((blocks, HD, rows), BF16),
            pltpu.VMEM((blocks, rows, HD), F32),
            pltpu.VMEM((blocks, rows, HD), F32),
        ],
        compiler_params=pltpu.CompilerParams(vmem_limit_bytes=48 << 20),
        name="attend",
    )(first, ends, q_loc, g_loc, kw, vw)


def scatter_kernel(
    nk, ns, o_ref, dq_ref, dkp, dvp, o_out, dq_out, dk_out, dv_out,
    held, summed, own_sem, send_kv, recv_kv, send_win, recv_win,
):
    me = lax.axis_index("kv")
    spot = lax.axis_index("seq")
    tok = o_out.shape[0]
    width = o_ref.shape[1]
    peers = [lax.rem(me + o, nk) for o in range(1, nk)]
    ahead = [lax.rem(spot + d, ns) for d in range(1, WIN + 1)]
    behind = [lax.rem(spot + ns - d, ns) for d in range(1, WIN + 1)]

    barrier = pltpu.get_barrier_semaphore()
    for peer in peers:
        pl.semaphore_signal(barrier, inc=1, device_id={"kv": peer}, device_id_type=MESH)
    for peer in ahead:
        pl.semaphore_signal(barrier, inc=1, device_id={"seq": peer}, device_id_type=MESH)
    pl.semaphore_wait(barrier, nk - 1 + WIN)

    far = []
    for a, part in enumerate((dkp, dvp)):
        for d in range(1, WIN + 1):
            copy = remote(
                part.at[WIN - d], held.at[a, d - 1], send_win.at[a, d - 1], recv_win.at[a, d - 1],
                {"seq": behind[d - 1]},
            )
            copy.start()
            far.append(copy)

    sends = []
    locals_ = []

    def spread(a, src, dst, size):
        def rows_of(to):
            return src.at[pl.ds(pl.multiple_of(to * tok, tok), tok), :]

        mine = dst.at[:, pl.ds(pl.multiple_of(me * size, size), size)]
        local = pltpu.make_async_copy(rows_of(me), mine, own_sem.at[a])
        local.start()
        locals_.append(local)
        for o, peer in enumerate(peers):
            copy = remote(rows_of(peer), mine, send_kv.at[a, o], recv_kv.at[a, o], {"kv": peer})
            copy.start()
            sends.append(copy)

    spread(0, o_ref, o_out, width)
    spread(1, dq_ref, dq_out, width)
    for a, (part, dst) in enumerate(((dkp, dk_out), (dvp, dv_out))):
        for copy in far[a * WIN:(a + 1) * WIN]:
            copy.wait_recv()
        total = part[WIN].astype(F32)
        for d in range(WIN):
            total = total + held[a, d].astype(F32)
        if a == 0:
            total = total * SCALE
        summed[a] = total.astype(BF16)
        spread(2 + a, summed.at[a], dst, HD)
    for local in locals_:
        local.wait()
    for copy in sends:
        copy.wait()
    for copy in far:
        copy.wait_send()


def scatter(o_loc, dq_loc, dkp, dvp):
    nk, ns = lax.axis_size("kv"), lax.axis_size("seq")
    rows, width = o_loc.shape
    tok = rows // nk
    return pl.pallas_call(
        functools.partial(scatter_kernel, nk, ns),
        out_shape=(
            jax.ShapeDtypeStruct((tok, width * nk), BF16),
            jax.ShapeDtypeStruct((tok, width * nk), BF16),
            jax.ShapeDtypeStruct((tok, HD * nk), BF16),
            jax.ShapeDtypeStruct((tok, HD * nk), BF16),
        ),
        in_specs=[vmem_spec()] * 4,
        out_specs=(any_spec(),) * 4,
        scratch_shapes=[
            pltpu.VMEM((2, WIN, rows, HD), BF16),
            pltpu.VMEM((2, rows, HD), BF16),
            pltpu.SemaphoreType.DMA((4,)),
            pltpu.SemaphoreType.DMA((4, nk - 1)),
            pltpu.SemaphoreType.DMA((4, nk - 1)),
            pltpu.SemaphoreType.DMA((2, WIN)),
            pltpu.SemaphoreType.DMA((2, WIN)),
        ],
        compiler_params=pltpu.CompilerParams(
            collective_id=1, has_side_effects=True, vmem_limit_bytes=48 << 20
        ),
        name="scatter",
    )(o_loc, dq_loc, dkp, dvp)


def body(queries, keys, values, grad_out, lengths):
    ends = jnp.cumsum(lengths).astype(jnp.int32)
    rows = queries.shape[0] * lax.axis_size("kv")
    first = (lax.axis_index("seq") * rows).astype(jnp.int32).reshape(1)
    q_loc, g_loc, kw, vw = gather(queries, keys, values, grad_out)
    o_loc, dq_loc, dkp, dvp = attend(q_loc, g_loc, kw, vw, first, ends)
    return scatter(o_loc, dq_loc, dkp, dvp)


def solution(mesh):
    split = P(("seq", "kv"), None)
    return jax.shard_map(
        body,
        mesh=mesh,
        in_specs=(split, split, split, split, P()),
        out_specs=(split, split, split, split),
        check_vma=False,
    )
```

```python
import functools

import jax
import jax.numpy as jnp
from jax import lax
from jax.experimental import pallas as pl
from jax.experimental.pallas import tpu as pltpu
from jax.sharding import PartitionSpec as P

HD = 128
GROUP = 8
WIN = 6
XS = 4
PIECES = 2
MESH = pl.DeviceIdType.MESH
SCALE = HD ** (-0.5)
SCALE2 = SCALE * 1.4426950408889634
MASKED = -1e30
F32 = jnp.float32
BF16 = jnp.bfloat16


def dot(a, b):
    return jnp.dot(a, b, preferred_element_type=F32)


def dot_nt(a, b):
    return lax.dot_general(a, b, (((1,), (1,)), ((), ())), preferred_element_type=F32)


def fold(x, op):
    rows, cols = x.shape
    return op(x.reshape(rows // 8, 8, cols), axis=0)


def span(i, size):
    return pl.ds(pl.multiple_of(i * size, size), size)


def kernel(
    nk, ns, lens_ref, q_ref, k_ref, v_ref, g_ref, o_out, dq_out, dk_out, dv_out,
    q_loc, g_loc, kwin, vwin, o_loc, dq_loc, part_k, part_v, held, moved, summed, final,
    bias, key_t, val_t, scores, probs, dscores, over, delta, qs, gs,
    own_sem, in_send, in_recv, win_send, win_recv, back_send, back_recv, out_send, out_recv,
):
    me = lax.axis_index("kv")
    spot = lax.axis_index("seq")
    col = lax.rem(spot, XS)
    tok = q_ref.shape[0]
    rows = tok * nk
    width = GROUP * HD
    peers = [lax.rem(me + o, nk) for o in range(1, nk)]

    def along(d):
        return {"seq": lax.rem(spot + ns + d, ns)}

    def beside(e):
        return {"seq": spot - col + lax.rem(col + XS + e, XS)}

    barrier = pltpu.get_barrier_semaphore()
    friends = [{"kv": p} for p in peers] + [beside(e) for e in (1, 2, 3)]
    friends += [along(s * d) for d in (1, 2, 3, 4, 8) for s in (1, -1)]
    for friend in friends:
        pl.semaphore_signal(barrier, inc=1, device_id=friend, device_id_type=MESH)
    pl.semaphore_wait(barrier, len(friends))

    def remote(src, dst, send, recv, peer):
        return pltpu.make_async_remote_copy(
            src_ref=src, dst_ref=dst, send_sem=send, recv_sem=recv, device_id=peer, device_id_type=MESH
        )

    pending, leaving = [], []


    def collect(a, src, dst, base, size):
        place = pl.ds(pl.multiple_of(base + me * tok, tok), tok)
        local = pltpu.make_async_copy(src.at[:, span(me, size)], dst.at[place, :], own_sem.at[a])
        local.start()
        got = [local]
        for o, peer in enumerate(peers):
            copy = remote(src.at[:, span(peer, size)], dst.at[place, :], in_send.at[a, o], in_recv.at[a, o], {"kv": peer})
            copy.start()
            leaving.append(copy)
            got.append(copy)
        return got

    def arrive(got):
        got[0].wait()
        for copy in got[1:]:
            copy.wait_recv()

    got_k = collect(0, k_ref, kwin, WIN * rows, HD)
    got_v = collect(1, v_ref, vwin, WIN * rows, HD)
    got_q = collect(2, q_ref, q_loc, 0, width)

    first = spot * rows
    query_pos = first + lax.broadcasted_iota(jnp.int32, (1, rows), 1)
    start = jnp.zeros((1, rows), jnp.int32)
    end = jnp.int32(0)
    for d in range(lens_ref.shape[0]):
        end = end + lens_ref[d]
        start = jnp.where(query_pos >= end, end, start)
    for b in range(WIN + 1):
        key_pos = first + (b - WIN) * rows + lax.broadcasted_iota(jnp.int32, (rows, rows), 0)
        allowed = key_pos >= start
        if b == WIN:
            allowed = allowed & (key_pos <= query_pos)
        bias[b] = jnp.where(allowed, 0.0, MASKED)

    def slot(win, i):
        return win.at[pl.ds(i * rows, rows), :]

    def share(a, win):
        copies = {}
        for d in (4, 8, 3, 2, 1):
            i = 7 if d == 8 else WIN - d
            copy = remote(slot(win, WIN), slot(win, i), win_send.at[a, i], win_recv.at[a, i], along(d))
            copies[d] = copy
            if d == 8:
                @pl.when(col >= 2)
                def _():
                    copy.start()
            else:
                copy.start()
        return copies

    def relay(a, win, copies):
        copies[4].wait_recv()

        @pl.when(col >= 2)
        def _():
            copies[8].wait_recv()

        for e in (2, 1):
            i = WIN - 4 - e
            from_slot = jnp.where(col + e >= XS, 7, WIN - 4)
            copy = remote(
                win.at[span(from_slot, rows), :], slot(win, i), win_send.at[a, i], win_recv.at[a, i], beside(e)
            )
            copy.start()
            copies[4 + e] = copy

    def landed(copies):
        for d in (1, 2, 3, 5, 6):
            copies[d].wait_recv()

    arrive(got_k)
    far_k = share(0, kwin)
    arrive(got_v)
    far_v = share(1, vwin)
    got_g = collect(3, g_ref, g_loc, 0, width)
    relay(0, kwin, far_k)
    relay(1, vwin, far_v)
    landed(far_k)
    arrive(got_q)

    def head(h):
        return span(h, HD)

    def score_step(h, carry):
        qh = q_loc[:, head(h)]
        top = jnp.full((8, rows), MASKED, F32)
        for b in range(WIN + 1):
            s = dot_nt(kwin[b * rows:(b + 1) * rows], qh) + bias[b]
            scores[b] = s
            top = jnp.maximum(top, fold(s, jnp.max))
        top = jnp.max(top, axis=0, keepdims=True) * SCALE2
        total = jnp.zeros((8, rows), F32)
        for b in range(WIN + 1):
            p = jnp.exp2(scores[b] * SCALE2 - top)
            total = total + fold(p, jnp.sum)
            probs[h, b * rows:(b + 1) * rows] = p.astype(BF16)
        over[pl.ds(h, 1), :] = 1.0 / jnp.sum(total, axis=0, keepdims=True)
        return carry

    lax.fori_loop(0, GROUP, score_step, 0)

    for b in range(WIN + 1):
        key_t[:, b * rows:(b + 1) * rows] = kwin[b * rows:(b + 1) * rows].T
    landed(far_v)
    for b in range(WIN + 1):
        val_t[:, b * rows:(b + 1) * rows] = vwin[b * rows:(b + 1) * rows].T
    arrive(got_g)

    def spread(a, src, dst, base, size, wide):
        def rows_of(to):
            return src.at[span(to, tok), pl.ds(base, size)]

        mine = dst.at[:, pl.ds(pl.multiple_of(me * wide + base, HD), size)]
        local = pltpu.make_async_copy(rows_of(me), mine, own_sem.at[4 + a])
        local.start()
        pending.append(local)
        for o, peer in enumerate(peers):
            copy = remote(rows_of(peer), mine, out_send.at[a, o], out_recv.at[a, o], {"kv": peer})
            copy.start()
            pending.append(copy)

    def out_step(h, carry):
        inv = over[pl.ds(h, 1), :]
        qh = q_loc[:, head(h)]
        gh = g_loc[:, head(h)]
        low = (dot(val_t[...], probs[h]) * inv).T.astype(BF16)
        o_loc[:, head(h)] = low
        delta[pl.ds(h, 1), :] = jnp.sum((gh.astype(F32) * low.astype(F32)).T, axis=0, keepdims=True)
        inv_col = jnp.broadcast_to(inv, (HD, rows)).T
        qs[span(h, rows), :] = (qh.astype(F32) * inv_col).astype(BF16)
        gs[span(h, rows), :] = (gh.astype(F32) * inv_col).astype(BF16)
        return carry

    each = GROUP // PIECES
    for i in range(PIECES):
        lax.fori_loop(i * each, (i + 1) * each, out_step, 0, unroll=2)
        spread(i, o_loc, o_out, i * each * HD, each * HD, width)

    back = {}

    def give(a, part, b):
        d = WIN - b
        peer = along(-d) if d <= 3 else beside(4 - d)
        copy = remote(part.at[b], held.at[a, b], back_send.at[a, b], back_recv.at[a, b], peer)
        copy.start()
        back[a, d] = copy

    def pass_on(a, part):
        back[a, 5].wait_recv()
        back[a, 6].wait_recv()
        far5, far6 = held[a, WIN - 5].astype(F32), held[a, WIN - 6].astype(F32)
        wrap5 = jnp.where(col >= 3, 1.0, 0.0)
        wrap6 = jnp.where(col >= 2, 1.0, 0.0)
        moved[a, 0] = (part[WIN - 4].astype(F32) + far5 * (1.0 - wrap5) + far6 * (1.0 - wrap6)).astype(BF16)
        moved[a, 1] = (far5 * wrap5 + far6 * wrap6).astype(BF16)
        i = WIN - 4
        copy = remote(moved.at[a, 0], held.at[a, i], back_send.at[a, i], back_recv.at[a, i], along(-4))
        copy.start()
        back[a, 4] = copy
        deep = remote(moved.at[a, 1], held.at[a, WIN], back_send.at[a, WIN], back_recv.at[a, WIN], along(-8))
        back[a, 8] = deep

        @pl.when(col >= 2)
        def _():
            deep.start()

    def finish(a, part, factor, dst):
        total = part[WIN].astype(F32)
        for d in (1, 2, 3, 4):
            back[a, d].wait_recv()
            total = total + held[a, WIN - d].astype(F32)
        summed[a] = total

        @pl.when(col >= 2)
        def _():
            back[a, 8].wait_recv()
            summed[a] = summed[a] + held[a, WIN].astype(F32)

        final[a] = (summed[a] * factor).astype(BF16)
        spread(2 * PIECES + a, final.at[a], dst, 0, HD, HD)

    for b in range(WIN + 1):
        block = slice(b * rows, (b + 1) * rows)

        def dv_step(h, acc):
            return acc + dot(probs[h, block], gs[span(h, rows), :])

        acc = lax.fori_loop(0, GROUP, dv_step, jnp.zeros((rows, HD), F32), unroll=True)
        part_v[b] = acc.astype(BF16)
        if b < WIN and b != WIN - 4:
            give(1, part_v, b)

    for b in range(WIN + 1):
        block = slice(b * rows, (b + 1) * rows)
        vb = vwin[block]

        def dk_step(h, acc):
            dp = dot_nt(vb, g_loc[:, head(h)])
            ds = (probs[h, block].astype(F32) * (dp - delta[pl.ds(h, 1), :])).astype(BF16)
            dscores[h, block] = ds
            return acc + dot(ds, qs[span(h, rows), :])

        acc = lax.fori_loop(0, GROUP, dk_step, jnp.zeros((rows, HD), F32), unroll=True)
        part_k[b] = acc.astype(BF16)
        if b < WIN and b != WIN - 4:
            give(0, part_k, b)
        if b == 2:
            pass_on(1, part_v)
    pass_on(0, part_k)

    def dq_step(h, carry):
        dq_t = dot(key_t[...], dscores[h])
        dq_loc[:, head(h)] = (dq_t * (over[pl.ds(h, 1), :] * SCALE)).T.astype(BF16)
        return carry

    for i in range(PIECES):
        lax.fori_loop(i * each, (i + 1) * each, dq_step, 0, unroll=2)
        spread(PIECES + i, dq_loc, dq_out, i * each * HD, each * HD, width)

    finish(1, part_v, 1.0, dv_out)
    finish(0, part_k, SCALE, dk_out)

    for copy in leaving:
        copy.wait_send()
    for copies in (far_k, far_v):
        for d, copy in copies.items():
            if d != 8:
                copy.wait_send()
    for (a, d), copy in back.items():
        if d != 8:
            copy.wait_send()

    @pl.when(col >= 2)
    def _():
        for copy in (far_k[8], far_v[8], back[0, 8], back[1, 8]):
            copy.wait_send()

    for copy in pending:
        copy.wait()


def body(queries, keys, values, grad_out, lengths):
    nk, ns = lax.axis_size("kv"), lax.axis_size("seq")
    tok = queries.shape[0]
    rows = tok * nk
    width = GROUP * HD
    blocks = WIN + 1
    whole = pl.BlockSpec(memory_space=pl.ANY)
    dma = pltpu.SemaphoreType.DMA
    return pl.pallas_call(
        functools.partial(kernel, nk, ns),
        out_shape=(
            jax.ShapeDtypeStruct(queries.shape, BF16),
            jax.ShapeDtypeStruct(queries.shape, BF16),
            jax.ShapeDtypeStruct(keys.shape, BF16),
            jax.ShapeDtypeStruct(keys.shape, BF16),
        ),
        in_specs=[pl.BlockSpec(memory_space=pltpu.SMEM)] + [whole] * 4,
        out_specs=(whole,) * 4,
        scratch_shapes=[
            pltpu.VMEM((rows, width), BF16),
            pltpu.VMEM((rows, width), BF16),
            pltpu.VMEM(((blocks + 1) * rows, HD), BF16),
            pltpu.VMEM(((blocks + 1) * rows, HD), BF16),
            pltpu.VMEM((rows, width), BF16),
            pltpu.VMEM((rows, width), BF16),
            pltpu.VMEM((blocks, rows, HD), BF16),
            pltpu.VMEM((blocks, rows, HD), BF16),
            pltpu.VMEM((2, blocks, rows, HD), BF16),
            pltpu.VMEM((2, 2, rows, HD), BF16),
            pltpu.VMEM((2, rows, HD), F32),
            pltpu.VMEM((2, rows, HD), BF16),
            pltpu.VMEM((blocks, rows, rows), F32),
            pltpu.VMEM((HD, blocks * rows), BF16),
            pltpu.VMEM((HD, blocks * rows), BF16),
            pltpu.VMEM((blocks, rows, rows), F32),
            pltpu.VMEM((GROUP, blocks * rows, rows), BF16),
            pltpu.VMEM((GROUP, blocks * rows, rows), BF16),
            pltpu.VMEM((GROUP, rows), F32),
            pltpu.VMEM((GROUP, rows), F32),
            pltpu.VMEM((GROUP * rows, HD), BF16),
            pltpu.VMEM((GROUP * rows, HD), BF16),
            dma((4 + 2 * PIECES + 2,)),
            dma((4, nk - 1)),
            dma((4, nk - 1)),
            dma((2, 8)),
            dma((2, 8)),
            dma((2, blocks)),
            dma((2, blocks)),
            dma((2 * PIECES + 2, nk - 1)),
            dma((2 * PIECES + 2, nk - 1)),
        ],
        compiler_params=pltpu.CompilerParams(
            collective_id=0, has_side_effects=True, vmem_limit_bytes=60 << 20
        ),
        name="attend",
    )(lengths, queries, keys, values, grad_out)


def solution(mesh):
    split = P(("seq", "kv"), None)
    return jax.shard_map(
        body,
        mesh=mesh,
        in_specs=(split, split, split, split, P()),
        out_specs=(split, split, split, split),
        check_vma=False,
    )
```

```python
import functools

import jax
import jax.numpy as jnp
from jax import lax
from jax.experimental import pallas as pl
from jax.experimental.pallas import tpu as pltpu
from jax.sharding import PartitionSpec as P

HD = 128
GROUP = 8
WIN = 6
XS = 4
CUTS = (0, 5, 8)
MESH = pl.DeviceIdType.MESH
SCALE = HD ** (-0.5)
SCALE2 = SCALE * 1.4426950408889634
MASKED = -1e30
F32 = jnp.float32
BF16 = jnp.bfloat16


def dot(a, b):
    return jnp.dot(a, b, preferred_element_type=F32)


def dot_nt(a, b):
    return lax.dot_general(a, b, (((1,), (1,)), ((), ())), preferred_element_type=F32)


def fold(x, op):
    rows, cols = x.shape
    return op(x.reshape(rows // 8, 8, cols), axis=0)


def span(i, size):
    return pl.ds(pl.multiple_of(i * size, size), size)


def kernel(
    nk, ns, lens_ref, q_ref, k_ref, v_ref, g_ref, o_out, dq_out, dk_out, dv_out,
    q_loc, g_loc, kwin, vwin, o_loc, dq_loc, part_k, part_v, held, moved, summed, final,
    bias, key_t, val_t, scores, tops, probs, dscores, over, delta, qs, gs,
    own_sem, in_send, in_recv, win_send, win_recv, back_send, back_recv, deep_send, deep_recv, out_send, out_recv,
):
    me = lax.axis_index("kv")
    spot = lax.axis_index("seq")
    col = lax.rem(spot, XS)
    tok = q_ref.shape[0]
    rows = tok * nk
    width = GROUP * HD
    peers = [lax.rem(me + o, nk) for o in range(1, nk)]

    def along(d):
        return {"seq": lax.rem(spot + ns + d, ns)}

    def beside(e):
        return {"seq": spot - col + lax.rem(col + XS + e, XS)}

    barrier = pltpu.get_barrier_semaphore()
    friends = [{"kv": p} for p in peers] + [beside(e) for e in (1, 2, 3)] + [along(XS), along(-XS)]
    for friend in friends:
        pl.semaphore_signal(barrier, inc=1, device_id=friend, device_id_type=MESH)
    pl.semaphore_wait(barrier, len(friends))

    def remote(src, dst, send, recv, peer):
        return pltpu.make_async_remote_copy(
            src_ref=src, dst_ref=dst, send_sem=send, recv_sem=recv, device_id=peer, device_id_type=MESH
        )

    pending, leaving = [], []


    def collect(a, src, dst, base, size):
        place = pl.ds(pl.multiple_of(base + me * tok, tok), tok)
        local = pltpu.make_async_copy(src.at[:, span(me, size)], dst.at[place, :], own_sem.at[a])
        local.start()
        for peer in peers:
            remote(
                src.at[:, span(peer, size)], dst.at[place, :], in_send.at[a], in_recv.at[a], {"kv": peer}
            ).start()
        n = nk - 1
        every = remote(
            src.at[:, pl.ds(0, n * size)], dst.at[pl.ds(base, n * tok), :], in_send.at[a], in_recv.at[a], {"kv": peers[0]}
        )
        leaving.append(every)
        return local, every

    def arrive(got):
        got[0].wait()
        got[1].wait_recv()

    got_k = collect(0, k_ref, kwin, WIN * rows, HD)
    got_v = collect(1, v_ref, vwin, WIN * rows, HD)
    got_q = collect(2, q_ref, q_loc, 0, width)
    got_g = collect(3, g_ref, g_loc, 0, width)

    first = spot * rows
    query_pos = first + lax.broadcasted_iota(jnp.int32, (1, rows), 1)
    start = jnp.zeros((1, rows), jnp.int32)
    end = jnp.int32(0)
    for d in range(lens_ref.shape[0]):
        end = end + lens_ref[d]
        start = jnp.where(query_pos >= end, end, start)
    for b in range(WIN + 1):
        key_pos = first + (b - WIN) * rows + lax.broadcasted_iota(jnp.int32, (rows, rows), 0)
        allowed = key_pos >= start
        if b == WIN:
            allowed = allowed & (key_pos <= query_pos)
        bias[b] = jnp.where(allowed, 0.0, MASKED)

    def slot(win, i):
        return win.at[pl.ds(i * rows, rows), :]

    def start_if(cond, copy):
        @pl.when(cond)
        def _():
            copy.start()

    def share(a, win):
        def hop(src, i, peer):
            return remote(src, slot(win, i), win_send.at[a, 1 if i == 7 else 0], win_recv.at[a, i], peer)

        copies = {4: hop(slot(win, WIN), WIN - 4, along(XS)), 8: hop(slot(win, WIN - 4), 7, along(XS))}
        for e in (2, 1, 3):
            near = jnp.where(col + e >= XS, WIN - 4, WIN)
            copies[e] = hop(win.at[span(near, rows), :], WIN - e, beside(e))
        for e in (2, 1):
            near = jnp.where(col + e >= XS, 7, WIN - 4)
            copies[4 + e] = hop(win.at[span(near, rows), :], WIN - 4 - e, beside(e))
        copies[4].start()
        for e in (2, 1, 3):
            start_if(col + e < XS, copies[e])
        return copies

    def relay(copies):
        copies[4].wait_recv()
        start_if(col >= 2, copies[8])
        for e in (2, 1, 3):
            start_if(col + e >= XS, copies[e])
        for e in (2, 1):
            start_if(col + e < XS, copies[4 + e])

    def relay_deep(copies):
        @pl.when(col >= 2)
        def _():
            copies[8].wait_recv()

        for e in (2, 1):
            start_if(col + e >= XS, copies[4 + e])

    def head(h):
        return span(h, HD)

    def score(b):
        block = slice(b * rows, (b + 1) * rows)

        def step(h, carry):
            s = dot_nt(kwin[block], q_loc[:, head(h)]) + bias[b]
            scores[h, block] = s
            top = fold(s, jnp.max)
            if b != WIN:
                top = jnp.maximum(top, tops[h])
            tops[h] = top
            return carry

        lax.fori_loop(0, GROUP, step, 0, unroll=4)

    arrive(got_k)
    far_k = share(0, kwin)
    arrive(got_v)
    far_v = share(1, vwin)
    relay(far_k)
    relay(far_v)
    arrive(got_q)
    score(WIN)
    relay_deep(far_k)
    relay_deep(far_v)
    for d in (1, 2, 3, 4, 5, 6):
        if d != 4:
            far_k[d].wait_recv()
        score(WIN - d)

    def weight_step(h, carry):
        top = jnp.max(tops[h], axis=0, keepdims=True) * SCALE2
        total = jnp.zeros((8, rows), F32)
        for b in range(WIN + 1):
            block = slice(b * rows, (b + 1) * rows)
            p = jnp.exp2(scores[h, block] * SCALE2 - top)
            total = total + fold(p, jnp.sum)
            probs[h, block] = p.astype(BF16)
        over[pl.ds(h, 1), :] = 1.0 / jnp.sum(total, axis=0, keepdims=True)
        return carry

    lax.fori_loop(0, GROUP, weight_step, 0)
    arrive(got_g)

    def scale_step(h, carry):
        inv_col = jnp.broadcast_to(over[pl.ds(h, 1), :], (HD, rows)).T
        qs[span(h, rows), :] = (q_loc[:, head(h)].astype(F32) * inv_col).astype(BF16)
        gs[span(h, rows), :] = (g_loc[:, head(h)].astype(F32) * inv_col).astype(BF16)
        return carry

    lax.fori_loop(0, GROUP, scale_step, 0, unroll=2)

    def spread(a, src, dst, base, size, wide):
        def rows_of(to):
            return src.at[span(to, tok), pl.ds(base, size)]

        mine = dst.at[:, pl.ds(pl.multiple_of(me * wide + base, HD), size)]
        local = pltpu.make_async_copy(rows_of(me), mine, own_sem.at[4 + a])
        local.start()
        pending.append(local)
        for peer in peers:
            remote(rows_of(peer), mine, out_send.at[a], out_recv.at[a], {"kv": peer}).start()
        n = nk - 1
        pending.append(
            remote(
                src.at[pl.ds(0, n * tok), pl.ds(base, size)], dst.at[:, pl.ds(0, n * size)],
                out_send.at[a], out_recv.at[a], {"kv": peers[0]},
            )
        )

    def out_step(h, carry):
        inv = over[pl.ds(h, 1), :]
        gh = g_loc[:, head(h)]
        low = (dot(val_t[...], probs[h]) * inv).T.astype(BF16)
        o_loc[:, head(h)] = low
        delta[pl.ds(h, 1), :] = jnp.sum((gh.astype(F32) * low.astype(F32)).T, axis=0, keepdims=True)
        return carry

    back = {}

    def give(a, part, b):
        d = WIN - b
        peer = beside(-d if d <= 3 else 4 - d)
        copy = remote(part.at[b], held.at[a, b], back_send.at[a], back_recv.at[a, b], peer)
        copy.start()
        back[a, d] = copy

    def send_on(a, i):
        copy = remote(moved.at[a, i], held.at[a, (WIN - 4, WIN)[i]], deep_send.at[a, i], deep_recv.at[a, i], along(-XS))
        back[a, (4, 8)[i]] = copy
        return copy

    def wrapped(e):
        return jnp.where(col + e >= XS, 1.0, 0.0)

    def pass_deep(a):
        back[a, 5].wait_recv()
        back[a, 6].wait_recv()
        deep = send_on(a, 1)

        @pl.when(col >= 2)
        def _():
            moved[a, 1] = (
                held[a, WIN - 5].astype(F32) * wrapped(1) + held[a, WIN - 6].astype(F32) * wrapped(2)
            ).astype(BF16)
            deep.start()

    def pass_on(a, part):
        total = part[WIN - 4].astype(F32)
        for e in (1, 2):
            total = total + held[a, WIN - 4 - e].astype(F32) * (1.0 - wrapped(e))
        for e in (1, 2, 3):
            back[a, e].wait_recv()
            total = total + held[a, WIN - e].astype(F32) * wrapped(e)
        summed[a] = total

        @pl.when(col >= 2)
        def _():
            back[a, 8].wait_recv()
            summed[a] = summed[a] + held[a, WIN].astype(F32)

        moved[a, 0] = summed[a].astype(BF16)
        send_on(a, 0).start()

    def finish(a, part, factor, dst):
        total = part[WIN].astype(F32)
        for e in (1, 2, 3):
            total = total + held[a, WIN - e].astype(F32) * (1.0 - wrapped(e))
        back[a, 4].wait_recv()
        total = total + held[a, WIN - 4].astype(F32)
        final[a] = (total * factor).astype(BF16)
        spread(len(CUTS) + a, final.at[a], dst, 0, HD, HD)

    order = (0, 1, 3, 4, 5, 2, 6)
    for b in order:
        block = slice(b * rows, (b + 1) * rows)

        def dv_step(h, acc):
            return acc + dot(probs[h, block], gs[span(h, rows), :])

        acc = lax.fori_loop(0, GROUP, dv_step, jnp.zeros((rows, HD), F32), unroll=True)
        part_v[b] = acc.astype(BF16)
        if b < WIN and b != WIN - 4:
            give(1, part_v, b)

    for d in (1, 2, 3, 5, 6):
        far_v[d].wait_recv()
    for b in range(WIN + 1):
        block = slice(b * rows, (b + 1) * rows)
        val_t[:, block] = vwin[block].T
    lax.fori_loop(0, GROUP, out_step, 0, unroll=2)
    spread(0, o_loc, o_out, 0, width, width)
    pass_deep(1)

    for b in order:
        block = slice(b * rows, (b + 1) * rows)
        vb = vwin[block]

        def dk_step(h, acc):
            dp = dot_nt(vb, g_loc[:, head(h)])
            ds = (probs[h, block].astype(F32) * (dp - delta[pl.ds(h, 1), :])).astype(BF16)
            dscores[h, block] = ds
            return acc + dot(ds, qs[span(h, rows), :])

        acc = lax.fori_loop(0, GROUP, dk_step, jnp.zeros((rows, HD), F32), unroll=True)
        part_k[b] = acc.astype(BF16)
        if b < WIN and b != WIN - 4:
            give(0, part_k, b)
        if b == 1:
            pass_on(1, part_v)
        if b == 2:
            pass_deep(0)
    finish(1, part_v, 1.0, dv_out)

    def dq_step(h, carry):
        dq_t = dot(key_t[...], dscores[h])
        dq_loc[:, head(h)] = (dq_t * (over[pl.ds(h, 1), :] * SCALE)).T.astype(BF16)
        return carry

    for b in range(WIN + 1):
        block = slice(b * rows, (b + 1) * rows)
        key_t[:, block] = kwin[block].T
    for i, (low, high) in enumerate(zip(CUTS, CUTS[1:])):
        lax.fori_loop(low, high, dq_step, 0, unroll=True)
        spread(1 + i, dq_loc, dq_out, low * HD, (high - low) * HD, width)
        if i == 0:
            pass_on(0, part_k)
    finish(0, part_k, SCALE, dk_out)

    for copy in leaving:
        copy.wait_send()
    for a, win in enumerate((kwin, vwin)):
        six = win.at[pl.ds(0, WIN * rows), :]
        remote(six, six, win_send.at[a, 0], win_recv.at[a, 0], along(XS)).wait_send()
    for a, part in enumerate((part_k, part_v)):
        five = part.at[pl.ds(0, WIN - 1)]
        remote(five, five, back_send.at[a], back_recv.at[a, 0], along(XS)).wait_send()
        back[a, 4].wait_send()

    @pl.when(col >= 2)
    def _():
        for copy in (far_k[8], far_v[8], back[0, 8], back[1, 8]):
            copy.wait_send()

    for copy in pending:
        copy.wait()


def hand_over(*refs):
    given, taken, held, sems = refs[:4], refs[4:8], refs[8:12], refs[12]
    come = [pltpu.make_async_copy(given[i], held[i], sems.at[0, i]) for i in range(4)]
    go = [pltpu.make_async_copy(held[i], taken[i], sems.at[1, i]) for i in range(4)]
    for copy in come:
        copy.start()
    for i in range(4):
        come[i].wait()
        go[i].start()
    for copy in go:
        copy.wait()


def body(queries, keys, values, grad_out, lengths):
    nk, ns = lax.axis_size("kv"), lax.axis_size("seq")
    tok = queries.shape[0]
    rows = tok * nk
    width = GROUP * HD
    blocks = WIN + 1
    whole = pl.BlockSpec(memory_space=pl.ANY)
    dma = pltpu.SemaphoreType.DMA
    results = pl.pallas_call(
        functools.partial(kernel, nk, ns),
        out_shape=(
            jax.ShapeDtypeStruct(queries.shape, BF16),
            jax.ShapeDtypeStruct(queries.shape, BF16),
            jax.ShapeDtypeStruct(keys.shape, BF16),
            jax.ShapeDtypeStruct(keys.shape, BF16),
        ),
        in_specs=[pl.BlockSpec(memory_space=pltpu.SMEM)] + [whole] * 4,
        out_specs=(whole,) * 4,
        scratch_shapes=[
            pltpu.VMEM((rows, width), BF16),
            pltpu.VMEM((rows, width), BF16),
            pltpu.VMEM(((blocks + 1) * rows, HD), BF16),
            pltpu.VMEM(((blocks + 1) * rows, HD), BF16),
            pltpu.VMEM((rows, width), BF16),
            pltpu.VMEM((rows, width), BF16),
            pltpu.VMEM((blocks, rows, HD), BF16),
            pltpu.VMEM((blocks, rows, HD), BF16),
            pltpu.VMEM((2, blocks, rows, HD), BF16),
            pltpu.VMEM((2, 2, rows, HD), BF16),
            pltpu.VMEM((2, rows, HD), F32),
            pltpu.VMEM((2, rows, HD), BF16),
            pltpu.VMEM((blocks, rows, rows), F32),
            pltpu.VMEM((HD, blocks * rows), BF16),
            pltpu.VMEM((HD, blocks * rows), BF16),
            pltpu.VMEM((GROUP, blocks * rows, rows), F32),
            pltpu.VMEM((GROUP, 8, rows), F32),
            pltpu.VMEM((GROUP, blocks * rows, rows), BF16),
            pltpu.VMEM((GROUP, blocks * rows, rows), BF16),
            pltpu.VMEM((GROUP, rows), F32),
            pltpu.VMEM((GROUP, rows), F32),
            pltpu.VMEM((GROUP * rows, HD), BF16),
            pltpu.VMEM((GROUP * rows, HD), BF16),
            dma((4 + len(CUTS) + 2,)),
            dma((4,)),
            dma((4,)),
            dma((2, 2)),
            dma((2, 8)),
            dma((2,)),
            dma((2, blocks)),
            dma((2, 2)),
            dma((2, 2)),
            dma((len(CUTS) + 2,)),
            dma((len(CUTS) + 2,)),
        ],
        compiler_params=pltpu.CompilerParams(
            collective_id=0, has_side_effects=True, vmem_limit_bytes=60 << 20
        ),
        name="attend",
    )(lengths, queries, keys, values, grad_out)
    return pl.pallas_call(
        hand_over,
        out_shape=tuple(jax.ShapeDtypeStruct(x.shape, x.dtype) for x in results),
        in_specs=[whole] * 4,
        out_specs=(whole,) * 4,
        scratch_shapes=[pltpu.VMEM(x.shape, x.dtype) for x in results] + [dma((2, 4))],
        compiler_params=pltpu.CompilerParams(vmem_limit_bytes=60 << 20),
        name="hand_over",
    )(*results)


def solution(mesh):
    split = P(("seq", "kv"), None)
    return jax.shard_map(
        body,
        mesh=mesh,
        in_specs=(split, split, split, split, P()),
        out_specs=(split, split, split, split),
        check_vma=False,
    )
```

```python
import functools

import jax
import jax.numpy as jnp
from jax import lax
from jax.experimental import pallas as pl
from jax.experimental.pallas import tpu as pltpu
from jax.sharding import PartitionSpec as P

HD = 128
GROUP = 8
WIN = 6
XS = 4
CUTS = (0, 4, 8)
MESH = pl.DeviceIdType.MESH
SCALE = HD ** (-0.5)
SCALE2 = SCALE * 1.4426950408889634
MASKED = -1e30
F32 = jnp.float32
BF16 = jnp.bfloat16


def dot(a, b):
    return jnp.dot(a, b, preferred_element_type=F32)


def dot_nt(a, b):
    return lax.dot_general(a, b, (((1,), (1,)), ((), ())), preferred_element_type=F32)


def fold(x, op):
    rows, cols = x.shape
    return op(x.reshape(rows // 8, 8, cols), axis=0)


def span(i, size):
    return pl.ds(pl.multiple_of(i * size, size), size)


def kernel(
    nk, ns, lens_ref, q_ref, k_ref, v_ref, g_ref, o_out, dq_out, dk_out, dv_out,
    q_loc, g_loc, kwin, vwin, o_loc, dq_loc, part_k, part_v, held, final,
    bias, key_t, val_t, scores, tops, probs, dscores, over, delta, qs, gs,
    own_sem, in_send, in_recv, win_send, win_recv, back_send, back_recv, out_send, out_recv,
):
    me = lax.axis_index("kv")
    spot = lax.axis_index("seq")
    col = lax.rem(spot, XS)
    tok = q_ref.shape[0]
    rows = tok * nk
    width = GROUP * HD
    peers = [lax.rem(me + o, nk) for o in range(1, nk)]

    def along(d):
        return {"seq": lax.rem(spot + ns + d, ns)}

    def beside(e):
        return {"seq": spot - col + lax.rem(col + XS + e, XS)}

    barrier = pltpu.get_barrier_semaphore()
    friends = [{"kv": p} for p in peers] + [beside(e) for e in (1, 2, 3)] + [along(XS), along(-XS)]
    for friend in friends:
        pl.semaphore_signal(barrier, inc=1, device_id=friend, device_id_type=MESH)
    pl.semaphore_wait(barrier, len(friends))

    def remote(src, dst, send, recv, peer):
        return pltpu.make_async_remote_copy(
            src_ref=src, dst_ref=dst, send_sem=send, recv_sem=recv, device_id=peer, device_id_type=MESH
        )

    pending, leaving = [], []


    def collect(a, src, dst, base, size):
        place = pl.ds(pl.multiple_of(base + me * tok, tok), tok)
        local = pltpu.make_async_copy(src.at[:, span(me, size)], dst.at[place, :], own_sem.at[a])
        local.start()
        for peer in peers:
            remote(
                src.at[:, span(peer, size)], dst.at[place, :], in_send.at[a], in_recv.at[a], {"kv": peer}
            ).start()
        n = nk - 1
        every = remote(
            src.at[:, pl.ds(0, n * size)], dst.at[pl.ds(base, n * tok), :], in_send.at[a], in_recv.at[a], {"kv": peers[0]}
        )
        leaving.append(every)
        return local, every

    def arrive(got):
        got[0].wait()
        got[1].wait_recv()

    got_k = collect(0, k_ref, kwin, WIN * rows, HD)
    got_v = collect(1, v_ref, vwin, WIN * rows, HD)
    got_q = collect(2, q_ref, q_loc, 0, width)
    got_g = collect(3, g_ref, g_loc, 0, width)

    first = spot * rows
    query_pos = first + lax.broadcasted_iota(jnp.int32, (1, rows), 1)
    start = jnp.zeros((1, rows), jnp.int32)
    end = jnp.int32(0)
    for d in range(lens_ref.shape[0]):
        end = end + lens_ref[d]
        start = jnp.where(query_pos >= end, end, start)
    for b in range(WIN + 1):
        key_pos = first + (b - WIN) * rows + lax.broadcasted_iota(jnp.int32, (rows, rows), 0)
        allowed = key_pos >= start
        if b == WIN:
            allowed = allowed & (key_pos <= query_pos)
        bias[b] = jnp.where(allowed, 0.0, MASKED)

    def slot(win, i):
        return win.at[pl.ds(i * rows, rows), :]

    def start_if(cond, copy):
        @pl.when(cond)
        def _():
            copy.start()

    def share(a, win):
        def hop(src, i, peer):
            return remote(src, slot(win, i), win_send.at[a], win_recv.at[a, i], peer)

        copies = {4: hop(slot(win, WIN), WIN - 4, along(XS))}
        for e in (1, 2, 3):
            near = jnp.where(col + e >= XS, WIN - 4, WIN)
            copies[e] = hop(win.at[span(near, rows), :], WIN - e, beside(e))
        for e in (1, 2):
            copies[4 + e] = hop(slot(win, WIN - e), WIN - 4 - e, along(XS))
        copies[4].start()
        return copies

    def share_beside(copies):
        for e in (2, 1, 3):
            start_if(col + e < XS, copies[e])

    def relay(copies):
        copies[4].wait_recv()
        for e in (2, 1, 3):
            start_if(col + e >= XS, copies[e])

    def relay_deep(copies):
        for e in (1, 2):
            copies[e].wait_recv()
            copies[4 + e].start()

    def head(h):
        return span(h, HD)

    def score(b):
        block = slice(b * rows, (b + 1) * rows)

        def step(h, carry):
            s = dot_nt(kwin[block], q_loc[:, head(h)]) + bias[b]
            scores[h, block] = s
            top = fold(s, jnp.max)
            if b != WIN:
                top = jnp.maximum(top, tops[h])
            tops[h] = top
            return carry

        lax.fori_loop(0, GROUP, step, 0, unroll=4)

    arrive(got_k)
    far_k = share(0, kwin)
    share_beside(far_k)
    arrive(got_v)
    far_v = share(1, vwin)
    relay(far_k)
    share_beside(far_v)
    relay_deep(far_k)
    arrive(got_q)
    score(WIN)
    relay(far_v)
    for d in (4, 1, 2, 3, 5, 6):
        if d in (3, 5, 6):
            far_k[d].wait_recv()
        score(WIN - d)
        if d == 3:
            relay_deep(far_v)

    def weight_step(h, carry):
        top = jnp.max(tops[h], axis=0, keepdims=True) * SCALE2
        total = jnp.zeros((8, rows), F32)
        for b in range(WIN + 1):
            block = slice(b * rows, (b + 1) * rows)
            p = jnp.exp2(scores[h, block] * SCALE2 - top)
            total = total + fold(p, jnp.sum)
            probs[h, block] = p.astype(BF16)
        over[pl.ds(h, 1), :] = 1.0 / jnp.sum(total, axis=0, keepdims=True)
        return carry

    lax.fori_loop(0, GROUP, weight_step, 0)
    arrive(got_g)

    def scale_step(h, carry):
        inv_col = jnp.broadcast_to(over[pl.ds(h, 1), :], (HD, rows)).T
        gs[span(h, rows), :] = (g_loc[:, head(h)].astype(F32) * inv_col).astype(BF16)
        return carry

    lax.fori_loop(0, GROUP, scale_step, 0, unroll=2)

    def spread(a, src, dst, base, size, wide):
        def rows_of(to):
            return src.at[span(to, tok), pl.ds(base, size)]

        mine = dst.at[:, pl.ds(pl.multiple_of(me * wide + base, HD), size)]
        local = pltpu.make_async_copy(rows_of(me), mine, own_sem.at[4 + a])
        local.start()
        pending.append(local)
        for peer in peers:
            remote(rows_of(peer), mine, out_send.at[a], out_recv.at[a], {"kv": peer}).start()
        n = nk - 1
        pending.append(
            remote(
                src.at[pl.ds(0, n * tok), pl.ds(base, size)], dst.at[:, pl.ds(0, n * size)],
                out_send.at[a], out_recv.at[a], {"kv": peers[0]},
            )
        )

    def out_step(h, carry):
        inv = over[pl.ds(h, 1), :]
        gh = g_loc[:, head(h)]
        low = (dot(val_t[...], probs[h]) * inv).T.astype(BF16)
        o_loc[:, head(h)] = low
        delta[pl.ds(h, 1), :] = jnp.sum((gh.astype(F32) * low.astype(F32)).T, axis=0, keepdims=True)
        inv_col = jnp.broadcast_to(inv, (HD, rows)).T
        qs[span(h, rows), :] = (q_loc[:, head(h)].astype(F32) * inv_col).astype(BF16)
        return carry

    back = {}

    def give(a, part, b):
        d = WIN - b
        peer = beside(-d) if d <= 3 else along(-XS)
        copy = remote(part.at[b], held.at[a, b], back_send.at[a], back_recv.at[a, b], peer)
        copy.start()
        back[a, d] = copy

    def gather_up(a, part, e):
        back[a, 4 + e].wait_recv()
        part[WIN - e] = (part[WIN - e].astype(F32) + held[a, WIN - 4 - e].astype(F32)).astype(BF16)
        give(a, part, WIN - e)

    def wrapped(e):
        return jnp.where(col + e >= XS, 1.0, 0.0)

    def pass_on(a, part):
        total = part[WIN - 4].astype(F32)
        for e in (1, 2, 3):
            back[a, e].wait_recv()
            total = total + held[a, WIN - e].astype(F32) * wrapped(e)
        part[WIN - 4] = total.astype(BF16)
        give(a, part, WIN - 4)

    def finish(a, part, factor, dst):
        total = part[WIN].astype(F32)
        for e in (1, 2, 3):
            total = total + held[a, WIN - e].astype(F32) * (1.0 - wrapped(e))
        back[a, 4].wait_recv()
        total = total + held[a, WIN - 4].astype(F32)
        final[a] = (total * factor).astype(BF16)
        spread(len(CUTS) + a, final.at[a], dst, 0, HD, HD)

    order = (0, 1, 3, 2, 4, 5, 6)
    for b in order:
        block = slice(b * rows, (b + 1) * rows)

        def dv_step(h, acc):
            return acc + dot(probs[h, block], gs[span(h, rows), :])

        acc = lax.fori_loop(0, GROUP, dv_step, jnp.zeros((rows, HD), F32), unroll=True)
        part_v[b] = acc.astype(BF16)
        if b in (0, 1, 3):
            give(1, part_v, b)

    for d in (3, 5, 6):
        far_v[d].wait_recv()
    for b in range(WIN + 1):
        block = slice(b * rows, (b + 1) * rows)
        val_t[:, block] = vwin[block].T
    lax.fori_loop(0, GROUP, out_step, 0, unroll=2)
    spread(0, o_loc, o_out, 0, width, width)

    for b in order:
        block = slice(b * rows, (b + 1) * rows)
        vb = vwin[block]

        def dk_step(h, acc):
            dp = dot_nt(vb, g_loc[:, head(h)])
            ds = (probs[h, block].astype(F32) * (dp - delta[pl.ds(h, 1), :])).astype(BF16)
            dscores[h, block] = ds
            return acc + dot(ds, qs[span(h, rows), :])

        acc = lax.fori_loop(0, GROUP, dk_step, jnp.zeros((rows, HD), F32), unroll=True)
        part_k[b] = acc.astype(BF16)
        if b in (0, 1, 3):
            give(0, part_k, b)
        if b == 0:
            gather_up(1, part_v, 2)
            gather_up(1, part_v, 1)
        if b in (4, 5):
            gather_up(0, part_k, WIN - b)
        if b == 5:
            pass_on(1, part_v)

    def dq_step(h, carry):
        dq_t = dot(key_t[...], dscores[h])
        dq_loc[:, head(h)] = (dq_t * (over[pl.ds(h, 1), :] * SCALE)).T.astype(BF16)
        return carry

    for b in range(WIN + 1):
        block = slice(b * rows, (b + 1) * rows)
        key_t[:, block] = kwin[block].T
    for i, (low, high) in enumerate(zip(CUTS, CUTS[1:])):
        lax.fori_loop(low, high, dq_step, 0, unroll=True)
        spread(1 + i, dq_loc, dq_out, low * HD, (high - low) * HD, width)
        if i == 0:
            pass_on(0, part_k)
            finish(1, part_v, 1.0, dv_out)
    finish(0, part_k, SCALE, dk_out)

    for copy in leaving:
        copy.wait_send()
    for a, win in enumerate((kwin, vwin)):
        six = win.at[pl.ds(0, WIN * rows), :]
        remote(six, six, win_send.at[a], win_recv.at[a, 0], along(XS)).wait_send()
    for a, part in enumerate((part_k, part_v)):
        six = part.at[pl.ds(0, WIN)]
        remote(six, six, back_send.at[a], back_recv.at[a, 0], along(XS)).wait_send()
    for copy in pending:
        copy.wait()


def hand_over(*refs):
    given, taken, held, sems = refs[:4], refs[4:8], refs[8:12], refs[12]
    come = [pltpu.make_async_copy(given[i], held[i], sems.at[0, i]) for i in range(4)]
    go = [pltpu.make_async_copy(held[i], taken[i], sems.at[1, i]) for i in range(4)]
    for copy in come:
        copy.start()
    for i in range(4):
        come[i].wait()
        go[i].start()
    for copy in go:
        copy.wait()


def body(queries, keys, values, grad_out, lengths):
    nk, ns = lax.axis_size("kv"), lax.axis_size("seq")
    tok = queries.shape[0]
    rows = tok * nk
    width = GROUP * HD
    blocks = WIN + 1
    whole = pl.BlockSpec(memory_space=pl.ANY)
    dma = pltpu.SemaphoreType.DMA
    results = pl.pallas_call(
        functools.partial(kernel, nk, ns),
        out_shape=(
            jax.ShapeDtypeStruct(queries.shape, BF16),
            jax.ShapeDtypeStruct(queries.shape, BF16),
            jax.ShapeDtypeStruct(keys.shape, BF16),
            jax.ShapeDtypeStruct(keys.shape, BF16),
        ),
        in_specs=[pl.BlockSpec(memory_space=pltpu.SMEM)] + [whole] * 4,
        out_specs=(whole,) * 4,
        scratch_shapes=[
            pltpu.VMEM((rows, width), BF16),
            pltpu.VMEM((rows, width), BF16),
            pltpu.VMEM((blocks * rows, HD), BF16),
            pltpu.VMEM((blocks * rows, HD), BF16),
            pltpu.VMEM((rows, width), BF16),
            pltpu.VMEM((rows, width), BF16),
            pltpu.VMEM((blocks, rows, HD), BF16),
            pltpu.VMEM((blocks, rows, HD), BF16),
            pltpu.VMEM((2, blocks, rows, HD), BF16),
            pltpu.VMEM((2, rows, HD), BF16),
            pltpu.VMEM((blocks, rows, rows), F32),
            pltpu.VMEM((HD, blocks * rows), BF16),
            pltpu.VMEM((HD, blocks * rows), BF16),
            pltpu.VMEM((GROUP, blocks * rows, rows), F32),
            pltpu.VMEM((GROUP, 8, rows), F32),
            pltpu.VMEM((GROUP, blocks * rows, rows), BF16),
            pltpu.VMEM((GROUP, blocks * rows, rows), BF16),
            pltpu.VMEM((GROUP, rows), F32),
            pltpu.VMEM((GROUP, rows), F32),
            pltpu.VMEM((GROUP * rows, HD), BF16),
            pltpu.VMEM((GROUP * rows, HD), BF16),
            dma((4 + len(CUTS) + 2,)),
            dma((4,)),
            dma((4,)),
            dma((2,)),
            dma((2, blocks)),
            dma((2,)),
            dma((2, blocks)),
            dma((len(CUTS) + 2,)),
            dma((len(CUTS) + 2,)),
        ],
        compiler_params=pltpu.CompilerParams(
            collective_id=0, has_side_effects=True, vmem_limit_bytes=60 << 20
        ),
        name="attend",
    )(lengths, queries, keys, values, grad_out)
    return pl.pallas_call(
        hand_over,
        out_shape=tuple(jax.ShapeDtypeStruct(x.shape, x.dtype) for x in results),
        in_specs=[whole] * 4,
        out_specs=(whole,) * 4,
        scratch_shapes=[pltpu.VMEM(x.shape, x.dtype) for x in results] + [dma((2, 4))],
        compiler_params=pltpu.CompilerParams(vmem_limit_bytes=60 << 20),
        name="hand_over",
    )(*results)


def solution(mesh):
    split = P(("seq", "kv"), None)
    return jax.shard_map(
        body,
        mesh=mesh,
        in_specs=(split, split, split, split, P()),
        out_specs=(split, split, split, split),
        check_vma=False,
    )
```

```python
import functools

import jax
import jax.numpy as jnp
from jax import lax
from jax.experimental import pallas as pl
from jax.experimental.pallas import tpu as pltpu
from jax.sharding import PartitionSpec as P

HD = 128
GROUP = 8
WIN = 6
XS = 4
CUTS = (0, 4, 8)
MESH = pl.DeviceIdType.MESH
SCALE = HD ** (-0.5)
SCALE2 = SCALE * 1.4426950408889634
MASKED = -1e30
F32 = jnp.float32
BF16 = jnp.bfloat16


def dot(a, b):
    return jnp.dot(a, b, preferred_element_type=F32)


def dot_nt(a, b):
    return lax.dot_general(a, b, (((1,), (1,)), ((), ())), preferred_element_type=F32)


def fold(x, op):
    rows, cols = x.shape
    return op(x.reshape(rows // 8, 8, cols), axis=0)


def span(i, size):
    return pl.ds(pl.multiple_of(i * size, size), size)


def kernel(
    nk, ns, lens_ref, q_ref, k_ref, v_ref, g_ref, o_out, dq_out, dk_out, dv_out,
    q_loc, g_loc, kwin, vwin, o_loc, dq_loc, part_k, part_v, held, final,
    bias, key_t, val_t, scores, tops, probs, dscores, over, delta, qs, sum_v,
    own_sem, in_send, in_recv, win_send, win_recv, back_send, back_recv, out_send, out_recv,
):
    me = lax.axis_index("kv")
    spot = lax.axis_index("seq")
    col = lax.rem(spot, XS)
    tok = q_ref.shape[0]
    rows = tok * nk
    width = GROUP * HD
    peers = [lax.rem(me + o, nk) for o in sorted(range(1, nk), key=lambda o: abs(o - nk // 2))]

    def along(d):
        return {"seq": lax.rem(spot + ns + d, ns)}

    def beside(e):
        return {"seq": spot - col + lax.rem(col + XS + e, XS)}

    barrier = pltpu.get_barrier_semaphore()
    friends = [{"kv": p} for p in peers] + [beside(e) for e in (1, 2, 3)] + [along(XS), along(-XS)]
    for friend in friends:
        pl.semaphore_signal(barrier, inc=1, device_id=friend, device_id_type=MESH)
    pl.semaphore_wait(barrier, len(friends))

    def remote(src, dst, send, recv, peer):
        return pltpu.make_async_remote_copy(
            src_ref=src, dst_ref=dst, send_sem=send, recv_sem=recv, device_id=peer, device_id_type=MESH
        )

    pending, leaving = [], []


    def collect(a, src, dst, base, size):
        place = pl.ds(pl.multiple_of(base + me * tok, tok), tok)
        local = pltpu.make_async_copy(src.at[:, span(me, size)], dst.at[place, :], own_sem.at[a])
        local.start()
        for peer in peers:
            remote(
                src.at[:, span(peer, size)], dst.at[place, :], in_send.at[a], in_recv.at[a], {"kv": peer}
            ).start()
        n = nk - 1
        every = remote(
            src.at[:, pl.ds(0, n * size)], dst.at[pl.ds(base, n * tok), :], in_send.at[a], in_recv.at[a], {"kv": peers[0]}
        )
        leaving.append(every)
        return local, every

    def arrive(got):
        got[0].wait()
        got[1].wait_recv()

    got_k = collect(0, k_ref, kwin, WIN * rows, HD)
    got_v = collect(1, v_ref, vwin, WIN * rows, HD)
    got_q = collect(2, q_ref, q_loc, 0, width)
    got_g = collect(3, g_ref, g_loc, 0, width)

    first = spot * rows
    query_pos = first + lax.broadcasted_iota(jnp.int32, (1, rows), 1)
    start = jnp.zeros((1, rows), jnp.int32)
    end = jnp.int32(0)
    for d in range(lens_ref.shape[0]):
        end = end + lens_ref[d]
        start = jnp.where(query_pos >= end, end, start)
    for b in range(WIN + 1):
        key_pos = first + (b - WIN) * rows + lax.broadcasted_iota(jnp.int32, (rows, rows), 0)
        allowed = key_pos >= start
        if b == WIN:
            allowed = allowed & (key_pos <= query_pos)
        bias[b] = jnp.where(allowed, 0.0, MASKED)

    def slot(win, i):
        return win.at[pl.ds(i * rows, rows), :]

    def start_if(cond, copy):
        @pl.when(cond)
        def _():
            copy.start()

    def share(a, win):
        def hop(src, i, peer):
            return remote(src, slot(win, i), win_send.at[a], win_recv.at[a, i], peer)

        copies = {4: hop(slot(win, WIN), WIN - 4, along(XS))}
        for e in (1, 2, 3):
            near = jnp.where(col + e >= XS, WIN - 4, WIN)
            copies[e] = hop(win.at[span(near, rows), :], WIN - e, beside(e))
        for e in (1, 2):
            copies[4 + e] = hop(slot(win, WIN - e), WIN - 4 - e, along(XS))
        copies[4].start()
        return copies

    def share_beside(copies):
        for e in (2, 1, 3):
            start_if(col + e < XS, copies[e])

    def relay(copies):
        copies[4].wait_recv()
        for e in (2, 1, 3):
            start_if(col + e >= XS, copies[e])

    def relay_deep(copies):
        for e in (1, 2):
            copies[e].wait_recv()
            copies[4 + e].start()

    def head(h):
        return span(h, HD)

    def score(b):
        block = slice(b * rows, (b + 1) * rows)

        def step(h, carry):
            s = dot_nt(kwin[block], q_loc[:, head(h)]) + bias[b]
            scores[h, block] = s
            top = fold(s, jnp.max)
            if b != WIN:
                top = jnp.maximum(top, tops[h])
            tops[h] = top
            return carry

        lax.fori_loop(0, GROUP, step, 0, unroll=4)

    arrive(got_k)
    far_k = share(0, kwin)
    share_beside(far_k)
    arrive(got_v)
    far_v = share(1, vwin)
    relay(far_k)
    share_beside(far_v)
    relay_deep(far_k)
    arrive(got_q)
    score(WIN)
    relay(far_v)
    for d in (4, 1, 2, 3, 5, 6):
        if d in (3, 5, 6):
            far_k[d].wait_recv()
        score(WIN - d)
        if d == 3:
            relay_deep(far_v)

    def spread(a, src, dst, base, size, wide):
        def rows_of(to):
            return src.at[span(to, tok), pl.ds(base, size)]

        mine = dst.at[:, pl.ds(pl.multiple_of(me * wide + base, HD), size)]
        local = pltpu.make_async_copy(rows_of(me), mine, own_sem.at[4 + a])
        local.start()
        pending.append(local)
        for peer in peers:
            remote(rows_of(peer), mine, out_send.at[a], out_recv.at[a], {"kv": peer}).start()
        n = nk - 1
        pending.append(
            remote(
                src.at[pl.ds(0, n * tok), pl.ds(base, size)], dst.at[:, pl.ds(0, n * size)],
                out_send.at[a], out_recv.at[a], {"kv": peers[0]},
            )
        )

    def out_step(h, carry):
        inv = over[pl.ds(h, 1), :]
        gh = g_loc[:, head(h)]
        low = (dot(val_t[...], probs[h]) * inv).T.astype(BF16)
        o_loc[:, head(h)] = low
        delta[pl.ds(h, 1), :] = jnp.sum((gh.astype(F32) * low.astype(F32)).T, axis=0, keepdims=True)
        inv_col = jnp.broadcast_to(inv, (HD, rows)).T
        qs[span(h, rows), :] = (q_loc[:, head(h)].astype(F32) * inv_col).astype(BF16)
        return carry

    back = {}

    def give(a, part, b):
        d = WIN - b
        peer = beside(-d) if d <= 3 else along(-XS)
        copy = remote(part.at[b], held.at[a, b], back_send.at[a], back_recv.at[a, b], peer)
        copy.start()
        back[a, d] = copy

    def gather_up(a, part, e):
        back[a, 4 + e].wait_recv()
        part[WIN - e] = (part[WIN - e].astype(F32) + held[a, WIN - 4 - e].astype(F32)).astype(BF16)
        give(a, part, WIN - e)

    def wrapped(e):
        return jnp.where(col + e >= XS, 1.0, 0.0)

    def pass_on(a, part):
        total = part[WIN - 4].astype(F32)
        for e in (1, 2, 3):
            back[a, e].wait_recv()
            total = total + held[a, WIN - e].astype(F32) * wrapped(e)
        part[WIN - 4] = total.astype(BF16)
        give(a, part, WIN - 4)

    def finish(a, part, factor, dst):
        total = part[WIN].astype(F32)
        for e in (1, 2, 3):
            total = total + held[a, WIN - e].astype(F32) * (1.0 - wrapped(e))
        back[a, 4].wait_recv()
        total = total + held[a, WIN - 4].astype(F32)
        final[a] = (total * factor).astype(BF16)
        spread(len(CUTS) + a, final.at[a], dst, 0, HD, HD)

    order = (0, 1, 3, 4, 5, 2, 6)
    arrive(got_g)
    for h in range(GROUP + 1):
        if h < GROUP:
            top = jnp.max(tops[h], axis=0, keepdims=True) * SCALE2
            total = jnp.zeros((8, rows), F32)
        if h > 0:
            inv_col = jnp.broadcast_to(over[h - 1:h, :], (HD, rows)).T
            gh = (g_loc[:, (h - 1) * HD:h * HD].astype(F32) * inv_col).astype(BF16)
        for b in range(WIN + 1):
            block = slice(b * rows, (b + 1) * rows)
            if h < GROUP:
                p = jnp.exp2(scores[h, block] * SCALE2 - top)
                total = total + fold(p, jnp.sum)
                probs[h, block] = p.astype(BF16)
            if h > 0:
                acc = dot(probs[h - 1, block], gh)
                if h > 1:
                    acc = acc + sum_v[b]
                if h < GROUP:
                    sum_v[b] = acc
                else:
                    part_v[b] = acc.astype(BF16)
        if h < GROUP:
            over[h:h + 1, :] = 1.0 / jnp.sum(total, axis=0, keepdims=True)
    for b in (0, 1, 3):
        give(1, part_v, b)

    for d in (3, 5, 6):
        far_v[d].wait_recv()
    for b in range(WIN + 1):
        block = slice(b * rows, (b + 1) * rows)
        val_t[:, block] = vwin[block].T
    lax.fori_loop(0, GROUP, out_step, 0, unroll=2)
    spread(0, o_loc, o_out, 0, width, width)

    for b in order:
        block = slice(b * rows, (b + 1) * rows)
        vb = vwin[block]

        def dk_step(h, acc):
            dp = dot_nt(vb, g_loc[:, head(h)])
            ds = (probs[h, block].astype(F32) * (dp - delta[pl.ds(h, 1), :])).astype(BF16)
            dscores[h, block] = ds
            return acc + dot(ds, qs[span(h, rows), :])

        acc = lax.fori_loop(0, GROUP, dk_step, jnp.zeros((rows, HD), F32), unroll=True)
        part_k[b] = acc.astype(BF16)
        if b in (0, 1, 3):
            give(0, part_k, b)
        if b == 0:
            gather_up(1, part_v, 2)
            gather_up(1, part_v, 1)
        if b in (4, 5):
            gather_up(0, part_k, WIN - b)
        if b == 2:
            pass_on(1, part_v)

    def dq_step(h, carry):
        dq_t = dot(key_t[...], dscores[h])
        dq_loc[:, head(h)] = (dq_t * (over[pl.ds(h, 1), :] * SCALE)).T.astype(BF16)
        return carry

    for b in range(WIN + 1):
        block = slice(b * rows, (b + 1) * rows)
        key_t[:, block] = kwin[block].T
    for i, (low, high) in enumerate(zip(CUTS, CUTS[1:])):
        lax.fori_loop(low, high, dq_step, 0, unroll=True)
        spread(1 + i, dq_loc, dq_out, low * HD, (high - low) * HD, width)
        if i == 0:
            pass_on(0, part_k)
    finish(1, part_v, 1.0, dv_out)
    finish(0, part_k, SCALE, dk_out)

    for copy in leaving:
        copy.wait_send()
    for a, win in enumerate((kwin, vwin)):
        six = win.at[pl.ds(0, WIN * rows), :]
        remote(six, six, win_send.at[a], win_recv.at[a, 0], along(XS)).wait_send()
    for a, part in enumerate((part_k, part_v)):
        six = part.at[pl.ds(0, WIN)]
        remote(six, six, back_send.at[a], back_recv.at[a, 0], along(XS)).wait_send()
    for copy in pending:
        copy.wait()


def hand_over(*refs):
    given, taken, held, sems = refs[:4], refs[4:8], refs[8:12], refs[12]
    come = [pltpu.make_async_copy(given[i], held[i], sems.at[0, i]) for i in range(4)]
    go = [pltpu.make_async_copy(held[i], taken[i], sems.at[1, i]) for i in range(4)]
    for copy in come:
        copy.start()
    for i in range(4):
        come[i].wait()
        go[i].start()
    for copy in go:
        copy.wait()


def body(queries, keys, values, grad_out, lengths):
    nk, ns = lax.axis_size("kv"), lax.axis_size("seq")
    tok = queries.shape[0]
    rows = tok * nk
    width = GROUP * HD
    blocks = WIN + 1
    whole = pl.BlockSpec(memory_space=pl.ANY)
    dma = pltpu.SemaphoreType.DMA
    results = pl.pallas_call(
        functools.partial(kernel, nk, ns),
        out_shape=(
            jax.ShapeDtypeStruct(queries.shape, BF16),
            jax.ShapeDtypeStruct(queries.shape, BF16),
            jax.ShapeDtypeStruct(keys.shape, BF16),
            jax.ShapeDtypeStruct(keys.shape, BF16),
        ),
        in_specs=[pl.BlockSpec(memory_space=pltpu.SMEM)] + [whole] * 4,
        out_specs=(whole,) * 4,
        scratch_shapes=[
            pltpu.VMEM((rows, width), BF16),
            pltpu.VMEM((rows, width), BF16),
            pltpu.VMEM((blocks * rows, HD), BF16),
            pltpu.VMEM((blocks * rows, HD), BF16),
            pltpu.VMEM((rows, width), BF16),
            pltpu.VMEM((rows, width), BF16),
            pltpu.VMEM((blocks, rows, HD), BF16),
            pltpu.VMEM((blocks, rows, HD), BF16),
            pltpu.VMEM((2, blocks, rows, HD), BF16),
            pltpu.VMEM((2, rows, HD), BF16),
            pltpu.VMEM((blocks, rows, rows), F32),
            pltpu.VMEM((HD, blocks * rows), BF16),
            pltpu.VMEM((HD, blocks * rows), BF16),
            pltpu.VMEM((GROUP, blocks * rows, rows), F32),
            pltpu.VMEM((GROUP, 8, rows), F32),
            pltpu.VMEM((GROUP, blocks * rows, rows), BF16),
            pltpu.VMEM((GROUP, blocks * rows, rows), BF16),
            pltpu.VMEM((GROUP, rows), F32),
            pltpu.VMEM((GROUP, rows), F32),
            pltpu.VMEM((GROUP * rows, HD), BF16),
            pltpu.VMEM((blocks, rows, HD), F32),
            dma((4 + len(CUTS) + 2,)),
            dma((4,)),
            dma((4,)),
            dma((2,)),
            dma((2, blocks)),
            dma((2,)),
            dma((2, blocks)),
            dma((len(CUTS) + 2,)),
            dma((len(CUTS) + 2,)),
        ],
        compiler_params=pltpu.CompilerParams(
            collective_id=0, has_side_effects=True, vmem_limit_bytes=60 << 20
        ),
        name="attend",
    )(lengths, queries, keys, values, grad_out)
    return pl.pallas_call(
        hand_over,
        out_shape=tuple(jax.ShapeDtypeStruct(x.shape, x.dtype) for x in results),
        in_specs=[whole] * 4,
        out_specs=(whole,) * 4,
        scratch_shapes=[pltpu.VMEM(x.shape, x.dtype) for x in results] + [dma((2, 4))],
        compiler_params=pltpu.CompilerParams(vmem_limit_bytes=60 << 20),
        name="hand_over",
    )(*results)


def solution(mesh):
    split = P(("seq", "kv"), None)
    return jax.shard_map(
        body,
        mesh=mesh,
        in_specs=(split, split, split, split, P()),
        out_specs=(split, split, split, split),
        check_vma=False,
    )
```

```python
import functools

import jax
import jax.numpy as jnp
from jax import lax
from jax.experimental import pallas as pl
from jax.experimental.pallas import tpu as pltpu
from jax.sharding import PartitionSpec as P

HD = 128
GROUP = 8
WIN = 6
XS = 4
CUTS = (0, 4, 8)
MESH = pl.DeviceIdType.MESH
SCALE = HD ** (-0.5)
SCALE2 = SCALE * 1.4426950408889634
MASKED = -1e30
F32 = jnp.float32
BF16 = jnp.bfloat16


def dot(a, b):
    return jnp.dot(a, b, preferred_element_type=F32)


def dot_nt(a, b):
    return lax.dot_general(a, b, (((1,), (1,)), ((), ())), preferred_element_type=F32)


def fold(x, op):
    rows, cols = x.shape
    return op(x.reshape(rows // 8, 8, cols), axis=0)


def span(i, size):
    return pl.ds(pl.multiple_of(i * size, size), size)


def kernel(
    nk, ns, lens_ref, q_ref, k_ref, v_ref, g_ref, o_out, dq_out, dk_out, dv_out,
    q_loc, g_loc, kwin, vwin, o_loc, dq_loc, part_k, part_v, held, final,
    bias, key_t, val_t, scores, tops, probs, dscores, over, delta, qs, sum_v,
    own_sem, in_send, in_recv, win_send, win_recv, back_send, back_recv, out_send, out_recv,
):
    me = lax.axis_index("kv")
    spot = lax.axis_index("seq")
    col = lax.rem(spot, XS)
    tok = q_ref.shape[0]
    rows = tok * nk
    width = GROUP * HD
    peers = [lax.rem(me + o, nk) for o in sorted(range(1, nk), key=lambda o: abs(o - nk // 2))]

    def along(d):
        return {"seq": lax.rem(spot + ns + d, ns)}

    def beside(e):
        return {"seq": spot - col + lax.rem(col + XS + e, XS)}

    barrier = pltpu.get_barrier_semaphore()
    friends = [{"kv": p} for p in peers] + [beside(e) for e in (1, 2, 3)] + [along(XS), along(-XS)]
    for friend in friends:
        pl.semaphore_signal(barrier, inc=1, device_id=friend, device_id_type=MESH)
    pl.semaphore_wait(barrier, len(friends))

    def remote(src, dst, send, recv, peer):
        return pltpu.make_async_remote_copy(
            src_ref=src, dst_ref=dst, send_sem=send, recv_sem=recv, device_id=peer, device_id_type=MESH
        )

    pending, leaving = [], []


    def collect(a, src, dst, base, size):
        place = pl.ds(pl.multiple_of(base + me * tok, tok), tok)
        local = pltpu.make_async_copy(src.at[:, span(me, size)], dst.at[place, :], own_sem.at[a])
        local.start()
        for peer in peers:
            remote(
                src.at[:, span(peer, size)], dst.at[place, :], in_send.at[a], in_recv.at[a], {"kv": peer}
            ).start()
        n = nk - 1
        every = remote(
            src.at[:, pl.ds(0, n * size)], dst.at[pl.ds(base, n * tok), :], in_send.at[a], in_recv.at[a], {"kv": peers[0]}
        )
        leaving.append(every)
        return local, every

    def arrive(got):
        got[0].wait()
        got[1].wait_recv()

    got_k = collect(0, k_ref, kwin, WIN * rows, HD)
    got_v = collect(1, v_ref, vwin, WIN * rows, HD)
    got_q = collect(2, q_ref, q_loc, 0, width)
    got_g = collect(3, g_ref, g_loc, 0, width)

    first = spot * rows
    query_pos = first + lax.broadcasted_iota(jnp.int32, (1, rows), 1)
    start = jnp.zeros((1, rows), jnp.int32)
    end = jnp.int32(0)
    for d in range(lens_ref.shape[0]):
        end = end + lens_ref[d]
        start = jnp.where(query_pos >= end, end, start)
    for b in range(WIN + 1):
        key_pos = first + (b - WIN) * rows + lax.broadcasted_iota(jnp.int32, (rows, rows), 0)
        allowed = key_pos >= start
        if b == WIN:
            allowed = allowed & (key_pos <= query_pos)
        bias[b] = jnp.where(allowed, 0.0, MASKED)

    def slot(win, i):
        return win.at[pl.ds(i * rows, rows), :]

    def start_if(cond, copy):
        @pl.when(cond)
        def _():
            copy.start()

    def share(a, win):
        def hop(src, i, peer):
            return remote(src, slot(win, i), win_send.at[a], win_recv.at[a, i], peer)

        copies = {4: hop(slot(win, WIN), WIN - 4, along(XS))}
        for e in (1, 2, 3):
            near = jnp.where(col + e >= XS, WIN - 4, WIN)
            copies[e] = hop(win.at[span(near, rows), :], WIN - e, beside(e))
        for e in (1, 2):
            copies[4 + e] = hop(slot(win, WIN - e), WIN - 4 - e, along(XS))
        copies[4].start()
        return copies

    def share_beside(copies):
        for e in (2, 1, 3):
            start_if(col + e < XS, copies[e])

    def relay(copies):
        copies[4].wait_recv()
        for e in (2, 1, 3):
            start_if(col + e >= XS, copies[e])

    def relay_deep(copies):
        for e in (1, 2):
            copies[e].wait_recv()
            copies[4 + e].start()

    def head(h):
        return span(h, HD)

    def score(b):
        block = slice(b * rows, (b + 1) * rows)

        def step(h, carry):
            s = dot_nt(kwin[block], q_loc[:, head(h)]) + bias[b]
            scores[h, block] = s
            top = fold(s, jnp.max)
            if b != WIN:
                top = jnp.maximum(top, tops[h])
            tops[h] = top
            return carry

        lax.fori_loop(0, GROUP, step, 0, unroll=4)

    arrive(got_k)
    far_k = share(0, kwin)
    share_beside(far_k)
    arrive(got_v)
    far_v = share(1, vwin)
    relay(far_k)
    share_beside(far_v)
    relay(far_v)
    relay_deep(far_k)
    arrive(got_q)
    score(WIN)
    for d in (4, 1, 2, 3, 5, 6):
        if d in (3, 5, 6):
            far_k[d].wait_recv()
        score(WIN - d)
        if d == 3:
            relay_deep(far_v)

    def spread(a, src, dst, base, size, wide):
        def rows_of(to):
            return src.at[span(to, tok), pl.ds(base, size)]

        mine = dst.at[:, pl.ds(pl.multiple_of(me * wide + base, HD), size)]
        local = pltpu.make_async_copy(rows_of(me), mine, own_sem.at[4 + a])
        local.start()
        pending.append(local)
        for peer in peers:
            remote(rows_of(peer), mine, out_send.at[a], out_recv.at[a], {"kv": peer}).start()
        n = nk - 1
        pending.append(
            remote(
                src.at[pl.ds(0, n * tok), pl.ds(base, size)], dst.at[:, pl.ds(0, n * size)],
                out_send.at[a], out_recv.at[a], {"kv": peers[0]},
            )
        )

    def out_step(h, carry):
        inv = over[pl.ds(h, 1), :]
        gh = g_loc[:, head(h)]
        low = (dot(val_t[...], probs[h]) * inv).T.astype(BF16)
        o_loc[:, head(h)] = low
        delta[pl.ds(h, 1), :] = jnp.sum((gh.astype(F32) * low.astype(F32)).T, axis=0, keepdims=True)
        inv_col = jnp.broadcast_to(inv, (HD, rows)).T
        qs[span(h, rows), :] = (q_loc[:, head(h)].astype(F32) * inv_col).astype(BF16)
        return carry

    back = {}

    def give(a, part, b):
        d = WIN - b
        peer = beside(-d) if d <= 3 else along(-XS)
        copy = remote(part.at[b], held.at[a, b], back_send.at[a], back_recv.at[a, b], peer)
        copy.start()
        back[a, d] = copy

    def gather_up(a, part, e):
        back[a, 4 + e].wait_recv()
        part[WIN - e] = (part[WIN - e].astype(F32) + held[a, WIN - 4 - e].astype(F32)).astype(BF16)
        give(a, part, WIN - e)

    def wrapped(e):
        return jnp.where(col + e >= XS, 1.0, 0.0)

    def pass_on(a, part):
        total = part[WIN - 4].astype(F32)
        for e in (1, 2, 3):
            back[a, e].wait_recv()
            total = total + held[a, WIN - e].astype(F32) * wrapped(e)
        part[WIN - 4] = total.astype(BF16)
        give(a, part, WIN - 4)

    def finish(a, part, factor, dst):
        total = part[WIN].astype(F32)
        for e in (1, 2, 3):
            total = total + held[a, WIN - e].astype(F32) * (1.0 - wrapped(e))
        back[a, 4].wait_recv()
        total = total + held[a, WIN - 4].astype(F32)
        final[a] = (total * factor).astype(BF16)
        spread(len(CUTS) + a, final.at[a], dst, 0, HD, HD)

    order = (0, 1, 3, 4, 5, 2, 6)
    arrive(got_g)
    for h in range(GROUP + 1):
        if h < GROUP:
            top = jnp.max(tops[h], axis=0, keepdims=True) * SCALE2
            total = jnp.zeros((8, rows), F32)
        if h > 0:
            inv_col = jnp.broadcast_to(over[h - 1:h, :], (HD, rows)).T
            gh = (g_loc[:, (h - 1) * HD:h * HD].astype(F32) * inv_col).astype(BF16)
        for b in range(WIN + 1):
            block = slice(b * rows, (b + 1) * rows)
            if h < GROUP:
                p = jnp.exp2(scores[h, block] * SCALE2 - top)
                total = total + fold(p, jnp.sum)
                probs[h, block] = p.astype(BF16)
            if h > 0:
                acc = dot(probs[h - 1, block], gh)
                if h > 1:
                    acc = acc + sum_v[b]
                if h < GROUP:
                    sum_v[b] = acc
                else:
                    part_v[b] = acc.astype(BF16)
        if h < GROUP:
            over[h:h + 1, :] = 1.0 / jnp.sum(total, axis=0, keepdims=True)
    for b in (0, 1, 3):
        give(1, part_v, b)

    for d in (3, 5, 6):
        far_v[d].wait_recv()
    for b in range(WIN + 1):
        block = slice(b * rows, (b + 1) * rows)
        val_t[:, block] = vwin[block].T
    lax.fori_loop(0, GROUP, out_step, 0, unroll=4)
    spread(0, o_loc, o_out, 0, width, width)

    for b in order:
        block = slice(b * rows, (b + 1) * rows)
        vb = vwin[block]

        def dk_step(h, acc):
            dp = dot_nt(vb, g_loc[:, head(h)])
            ds = (probs[h, block].astype(F32) * (dp - delta[pl.ds(h, 1), :])).astype(BF16)
            dscores[h, block] = ds
            return acc + dot(ds, qs[span(h, rows), :])

        acc = lax.fori_loop(0, GROUP, dk_step, jnp.zeros((rows, HD), F32), unroll=True)
        part_k[b] = acc.astype(BF16)
        if b in (0, 1, 3):
            give(0, part_k, b)
        if b == 0:
            gather_up(1, part_v, 2)
            gather_up(1, part_v, 1)
        if b in (4, 5):
            gather_up(0, part_k, WIN - b)
        if b == 2:
            pass_on(1, part_v)

    def dq_step(h, carry):
        dq_t = dot(key_t[...], dscores[h])
        dq_loc[:, head(h)] = (dq_t * (over[pl.ds(h, 1), :] * SCALE)).T.astype(BF16)
        return carry

    for b in range(WIN + 1):
        block = slice(b * rows, (b + 1) * rows)
        key_t[:, block] = kwin[block].T
    for i, (low, high) in enumerate(zip(CUTS, CUTS[1:])):
        lax.fori_loop(low, high, dq_step, 0, unroll=True)
        if i == 0:
            pass_on(0, part_k)
        spread(1 + i, dq_loc, dq_out, low * HD, (high - low) * HD, width)
    finish(0, part_k, SCALE, dk_out)
    finish(1, part_v, 1.0, dv_out)

    for copy in leaving:
        copy.wait_send()
    for a, win in enumerate((kwin, vwin)):
        six = win.at[pl.ds(0, WIN * rows), :]
        remote(six, six, win_send.at[a], win_recv.at[a, 0], along(XS)).wait_send()
    for a, part in enumerate((part_k, part_v)):
        six = part.at[pl.ds(0, WIN)]
        remote(six, six, back_send.at[a], back_recv.at[a, 0], along(XS)).wait_send()
    for copy in pending:
        copy.wait()


def hand_over(*refs):
    given, taken, held, sems = refs[:4], refs[4:8], refs[8:12], refs[12]
    come = [pltpu.make_async_copy(given[i], held[i], sems.at[0, i]) for i in range(4)]
    go = [pltpu.make_async_copy(held[i], taken[i], sems.at[1, i]) for i in range(4)]
    for copy in come:
        copy.start()
    for i in range(4):
        come[i].wait()
        go[i].start()
    for copy in go:
        copy.wait()


def body(queries, keys, values, grad_out, lengths):
    nk, ns = lax.axis_size("kv"), lax.axis_size("seq")
    tok = queries.shape[0]
    rows = tok * nk
    width = GROUP * HD
    blocks = WIN + 1
    whole = pl.BlockSpec(memory_space=pl.ANY)
    dma = pltpu.SemaphoreType.DMA
    results = pl.pallas_call(
        functools.partial(kernel, nk, ns),
        out_shape=(
            jax.ShapeDtypeStruct(queries.shape, BF16),
            jax.ShapeDtypeStruct(queries.shape, BF16),
            jax.ShapeDtypeStruct(keys.shape, BF16),
            jax.ShapeDtypeStruct(keys.shape, BF16),
        ),
        in_specs=[pl.BlockSpec(memory_space=pltpu.SMEM)] + [whole] * 4,
        out_specs=(whole,) * 4,
        scratch_shapes=[
            pltpu.VMEM((rows, width), BF16),
            pltpu.VMEM((rows, width), BF16),
            pltpu.VMEM((blocks * rows, HD), BF16),
            pltpu.VMEM((blocks * rows, HD), BF16),
            pltpu.VMEM((rows, width), BF16),
            pltpu.VMEM((rows, width), BF16),
            pltpu.VMEM((blocks, rows, HD), BF16),
            pltpu.VMEM((blocks, rows, HD), BF16),
            pltpu.VMEM((2, blocks, rows, HD), BF16),
            pltpu.VMEM((2, rows, HD), BF16),
            pltpu.VMEM((blocks, rows, rows), F32),
            pltpu.VMEM((HD, blocks * rows), BF16),
            pltpu.VMEM((HD, blocks * rows), BF16),
            pltpu.VMEM((GROUP, blocks * rows, rows), F32),
            pltpu.VMEM((GROUP, 8, rows), F32),
            pltpu.VMEM((GROUP, blocks * rows, rows), BF16),
            pltpu.VMEM((GROUP, blocks * rows, rows), BF16),
            pltpu.VMEM((GROUP, rows), F32),
            pltpu.VMEM((GROUP, rows), F32),
            pltpu.VMEM((GROUP * rows, HD), BF16),
            pltpu.VMEM((blocks, rows, HD), F32),
            dma((4 + len(CUTS) + 2,)),
            dma((4,)),
            dma((4,)),
            dma((2,)),
            dma((2, blocks)),
            dma((2,)),
            dma((2, blocks)),
            dma((len(CUTS) + 2,)),
            dma((len(CUTS) + 2,)),
        ],
        compiler_params=pltpu.CompilerParams(
            collective_id=0, has_side_effects=True, vmem_limit_bytes=60 << 20
        ),
        name="attend",
    )(lengths, queries, keys, values, grad_out)
    return pl.pallas_call(
        hand_over,
        out_shape=tuple(jax.ShapeDtypeStruct(x.shape, x.dtype) for x in results),
        in_specs=[whole] * 4,
        out_specs=(whole,) * 4,
        scratch_shapes=[pltpu.VMEM(x.shape, x.dtype) for x in results] + [dma((2, 4))],
        compiler_params=pltpu.CompilerParams(vmem_limit_bytes=60 << 20),
        name="hand_over",
    )(*results)


def solution(mesh):
    split = P(("seq", "kv"), None)
    return jax.shard_map(
        body,
        mesh=mesh,
        in_specs=(split, split, split, split, P()),
        out_specs=(split, split, split, split),
        check_vma=False,
    )
```
